512 devices in a mesh: dp: 32 (over x, y), seq: 16 (over z, core).
Axes of the slice: x: 4, y: 8, z: 8, core: 2. Of those that a mesh axis runs over, the one named last changes fastest.
Arguments:
- tri_query: bfloat16 [65536, 2048], P(('dp', 'seq')), parts along dimension 0, may hold values from -52 to 52
- tri_keys: bfloat16 [65536, 512], P(('dp', 'seq')), parts along dimension 0, may hold values from -4 to 4
- att_query: bfloat16 [65536, 2048], P(('dp', 'seq')), parts along dimension 0, may hold values from -52 to 52
- norm_gain: float32 [2048], replicated, may hold values from 0.1 to 1.9
- kv_weight: bfloat16 [2048, 256], replicated, may hold values from -0.125 to 0.125
Outputs:
- tri_out: bfloat16 [65536, 2048], P(('dp', 'seq')), parts along dimension 0
- attended: bfloat16 [65536, 2048], P(('dp', 'seq')), parts along dimension 0
The draws below stay inside these ranges and needn't reach their ends.
There are 32 independent parts, one for each index of `dp`. The reference program is written for one: setup_inputs(seed, part) draws one part's arguments, and reference() takes and returns one part's arrays. A program takes and returns all parts, laid end to end along the dimension named above; an argument that names none is the same for every part. Nothing has to cross between parts.
All inputs are finite; a program needn't handle non-finite values.
Results may differ from the reference program's by a relative error of at most 0.019.
The reference program's roundings to bfloat16 on the way count: a program that leaves them out, or rounds other values in their place, can miss the bound.
Values may be sent and summed in bfloat16 or wider, within the bound.
No kernel may reach another device: no remote copies, remote signals or barrier semaphores. Data moves between devices by JAX's collectives and lax.ppermute only.
A program may use at most 64 MiB of HBM per device.

```python
import jax
import jax.numpy as jnp
from jax import lax

HEADS = 16
HEAD_DIM = 128
W1 = 128
W2 = 16
TOKENS = 2048


def draw_tri_query(key, part):
    key = jax.random.fold_in(key, 1)
    return jnp.clip(jax.random.normal(key, (TOKENS, HEADS * HEAD_DIM), jnp.float32), -4.0, 4.0).astype(jnp.bfloat16)


def draw_att_query(key, part):
    key = jax.random.fold_in(key, 2)
    return jnp.clip(jax.random.normal(key, (TOKENS, HEADS * HEAD_DIM), jnp.float32), -4.0, 4.0).astype(jnp.bfloat16)


def shard_levels(stream_key, dims, pieces, smallest, high):
    level = 1.0
    for dim, blocks in pieces:
        draws = jax.random.uniform(jax.random.fold_in(jax.random.fold_in(stream_key, 6), dim), (blocks,), jnp.float32, smallest / len(pieces), high / len(pieces))
        level = level * jnp.repeat(jnp.exp(draws), dims[dim] // blocks).reshape((-1,) + (1,) * (len(dims) - 1 - dim))
    return level


def bell_draw(rng, extent, width, bound, pieces=(), kind=jnp.bfloat16):
    gain = shard_levels(rng, extent, pieces, -0.22, 0.18) if pieces else 1.0
    array = jax.random.normal(rng, extent, jnp.float32) * width * gain
    return jnp.minimum(jnp.maximum(array, -bound), bound).astype(kind)


def setup_inputs(seed: int = 0, part: int = 0) -> dict:
    streams_of = jax.random.split(jax.random.key(seed), 6)
    part_keys = jax.random.split(jax.random.fold_in(streams_of[5], part), 6)
    return {
        "tri_query": draw_tri_query(jax.random.fold_in(jax.random.fold_in(streams_of[5], part), 71), part),
        "tri_keys": bell_draw(part_keys[1], (TOKENS, 4 * HEAD_DIM), 1.0, 4.0, ((0, 16),)),
        "att_query": draw_att_query(jax.random.fold_in(jax.random.fold_in(streams_of[5], part), 71), part),
        "norm_gain": jnp.clip(1.0 + 0.18 * jax.random.normal(streams_of[3], (HEADS * HEAD_DIM,), jnp.float32), 0.1, 1.9),
        "kv_weight": bell_draw(streams_of[4], (HEADS * HEAD_DIM, 2 * HEAD_DIM), (HEADS * HEAD_DIM) ** -0.5, 0.125),
    }


NEG = -1e+30

def tri_block(query_rows, window, first_pos):
    head_width = window.shape[1] // 4
    row_count = query_rows.shape[0]
    head_count = query_rows.shape[1] // head_width
    scale = head_width ** (-0.5)
    key_one = window[:, :head_width].astype(jnp.float32)
    val_one = window[:, head_width:2 * head_width].astype(jnp.float32)
    key_two = jnp.stack([window[row_count - delay:2 * row_count - delay, 2 * head_width:3 * head_width] for delay in range(W2)]).astype(jnp.float32)
    val_two = jnp.stack([window[row_count - delay:2 * row_count - delay, 3 * head_width:] for delay in range(W2)]).astype(jnp.float32)
    query_pos = first_pos + jnp.arange(row_count, dtype=jnp.int32)
    key_pos = first_pos - row_count + jnp.arange(2 * row_count, dtype=jnp.int32)
    distance = jnp.arange(2 * row_count, dtype=jnp.int32)[None, :] - jnp.arange(row_count, dtype=jnp.int32)[:, None]
    inside = (distance >= 1) & (distance <= row_count) & (key_pos[None, :] >= 0)
    lagged = query_pos[None, :] - jnp.arange(W2, dtype=jnp.int32)[:, None]
    allowed = inside[None, :, :] & (lagged >= 0)[:, :, None]
    per_head = query_rows.reshape(row_count, head_count, head_width).transpose(1, 0, 2)

    def one_head(query):
        mixed_q = (query.astype(jnp.float32)[None] * key_two).astype(jnp.bfloat16)
        mixed_q = lax.optimization_barrier(mixed_q).astype(jnp.float32)
        score = jnp.einsum('oad,rd->oar', mixed_q, key_one) * scale
        row_top = lax.optimization_barrier(jnp.max(jnp.where(allowed, score, NEG), axis=(0, 2)))
        weight = jnp.where(allowed, jnp.exp(score - row_top[None, :, None]), 0.0)
        row_total = lax.optimization_barrier(jnp.sum(weight, axis=(0, 2)))
        rounded = lax.optimization_barrier(weight.astype(jnp.bfloat16)).astype(jnp.float32)
        paired = jnp.einsum('oar,rd->oad', rounded, val_one)
        return lax.optimization_barrier(jnp.sum(val_two * paired, axis=0)) / row_total[:, None]
    result = lax.map(one_head, per_head)
    return result.transpose(1, 0, 2).reshape(row_count, head_count * head_width).astype(jnp.bfloat16)

def reference(tri_query, tri_keys, att_query, norm_gain, kv_weight):
    padded = jnp.concatenate([jnp.zeros((W1, tri_keys.shape[1]), tri_keys.dtype), tri_keys], 0)

    def do_block(number):
        begin_at = (number * W1).astype(jnp.int32)
        query = lax.dynamic_slice_in_dim(tri_query, begin_at, W1, 0)
        window = lax.dynamic_slice_in_dim(padded, begin_at, 2 * W1, 0)
        return tri_block(query, window, begin_at)
    tri_out = lax.map(do_block, jnp.arange(TOKENS // W1, dtype=jnp.int32)).reshape(TOKENS, HEADS * HEAD_DIM)
    widened = tri_out.astype(jnp.float32)
    normed = (widened * lax.rsqrt(lax.optimization_barrier(jnp.mean(widened * widened, -1, keepdims=True)) + 1e-06) * norm_gain.astype(jnp.float32)).astype(jnp.bfloat16)
    key_vals = jnp.dot(normed, kv_weight, preferred_element_type=jnp.float32).astype(jnp.bfloat16)
    key_rows = key_vals[:, :HEAD_DIM]
    val_rows = key_vals[:, HEAD_DIM:]
    positions = jnp.arange(TOKENS, dtype=jnp.int32)
    causal = positions[None, :] <= positions[:, None]
    scale = HEAD_DIM ** (-0.5)
    per_head = att_query.reshape(TOKENS, HEADS, HEAD_DIM).transpose(1, 0, 2)

    def one_head(query):
        score = jnp.dot(query, key_rows.T, preferred_element_type=jnp.float32) * scale
        row_top = lax.optimization_barrier(jnp.max(jnp.where(causal, score, NEG), -1))
        weight = jnp.where(causal, jnp.exp(score - row_top[:, None]), 0.0)
        row_total = lax.optimization_barrier(jnp.sum(weight, -1))
        return jnp.dot(weight.astype(jnp.bfloat16), val_rows, preferred_element_type=jnp.float32) / row_total[:, None]
    attended = lax.map(one_head, per_head).transpose(1, 0, 2).reshape(TOKENS, HEADS * HEAD_DIM).astype(jnp.bfloat16)
    return (tri_out, attended)
```

```python
import functools

import jax
import jax.numpy as jnp
from jax import lax
from jax.experimental import pallas as pl
from jax.experimental.pallas import tpu as pltpu
from jax.sharding import PartitionSpec as P

HEADS = 16
DIM = 128
W1 = 128
W2 = 16
NEG = -1e30
SCALE = DIM**-0.5
EXP2_SCALE = SCALE * 1.4426950408889634
NT = (((1,), (1,)), ((), ()))


def tri_kernel(
    me_ref, q_ref, prev_ref, cur_ref, gain_ref, weight_ref, held_ref, out_ref, kv_ref,
    k2_scr, v2_scr, mask_scr, mq_scr, s_scr, normed_scr, shift_scr, *, first_row, rows,
):
    first_shard = me_ref[0] == 0

    shift_scr[0:16, :] = prev_ref[W1 - 16 : W1, 2 * DIM :].astype(jnp.float32)
    shift_scr[16:, :] = cur_ref[:, 2 * DIM :].astype(jnp.float32)
    for lag in range(W2):
        at = 16 + first_row - lag
        k2_scr[lag] = shift_scr[at : at + rows, :DIM].astype(jnp.bfloat16)
        v2_scr[lag] = shift_scr[at : at + rows, DIM:]
    row = first_row + lax.broadcasted_iota(jnp.int32, (rows, DIM), 0)
    col = lax.broadcasted_iota(jnp.int32, (rows, DIM), 1)
    own = col <= row
    mask_scr[0] = jnp.where(own, 1.0, 0.0).astype(jnp.bfloat16)
    k1 = jnp.concatenate([cur_ref[:, :DIM], prev_ref[:, :DIM]], 0)
    v1 = jnp.concatenate([cur_ref[:, DIM : 2 * DIM], prev_ref[:, DIM : 2 * DIM]], 0)

    def one_head(head, square, first):
        lanes = pl.ds(pl.multiple_of(head * DIM, DIM), DIM)
        query = q_ref[:, lanes]
        mq = (query[None] * k2_scr[...]).reshape(W2 * rows, DIM)
        both = lax.dot_general(mq, k1, NT, preferred_element_type=jnp.float32)
        both = both.reshape(W2, rows, 2 * DIM)
        if first:
            score = jnp.where(own[None], both[:, :, :DIM], NEG)
            if first_row < W2:
                lag = lax.broadcasted_iota(jnp.int32, (W2, rows, DIM), 0)
                score = jnp.where(lag <= row[None], score, NEG)
        else:
            score = jnp.where(own[None], both[:, :, :DIM], both[:, :, DIM:])
        s_scr[...] = score
        top = jnp.max(jnp.max(score, axis=0), axis=-1, keepdims=True)
        weight = jnp.exp2((s_scr[...] - top[None]) * EXP2_SCALE)
        total = jnp.sum(jnp.sum(weight, axis=0), axis=-1, keepdims=True)
        rounded = weight.astype(jnp.bfloat16)
        w_own = rounded * mask_scr[...]
        w_prev = rounded - w_own
        halves = jnp.concatenate([w_own, w_prev], -1).reshape(W2 * rows, 2 * DIM)
        paired = jnp.dot(halves, v1, preferred_element_type=jnp.float32)
        result = jnp.sum(paired.reshape(W2, rows, DIM) * v2_scr[...], axis=0) / total
        result = result.astype(jnp.bfloat16)
        out_ref[:, lanes] = result
        wide = result.astype(jnp.float32)
        return square + wide * wide

    def finish(square):
        mean = jnp.sum(square, axis=-1, keepdims=True) * (1.0 / (HEADS * DIM))
        inverse = lax.rsqrt(mean + 1e-6)
        normed = (out_ref[...].astype(jnp.float32) * inverse * gain_ref[...]).astype(jnp.bfloat16)
        kv_ref[...] = jnp.dot(
            normed, weight_ref[...], preferred_element_type=jnp.float32
        ).astype(jnp.bfloat16)

    zero = jnp.zeros((rows, DIM), jnp.float32)

    @pl.when(first_shard)
    def _():
        finish(lax.fori_loop(0, HEADS, lambda h, sq: one_head(h, sq, True), zero))

    @pl.when(jnp.logical_not(first_shard))
    def _():
        finish(lax.fori_loop(0, HEADS, lambda h, sq: one_head(h, sq, False), zero))


def tri_call(me, tri_query, behind, tri_keys, gain, kv_weight, held, number, rows):
    token_rows, width = tri_query.shape
    whole = lambda shape: pl.BlockSpec(shape, lambda i: (0,) * len(shape))
    in_specs = [
        pl.BlockSpec(memory_space=pltpu.SMEM),
        pl.BlockSpec((rows, width), lambda i: (number, 0)),
        whole(behind.shape),
        whole(tri_keys.shape),
        whole(gain.shape),
        whole(kv_weight.shape),
    ]
    args = [me, tri_query, behind, tri_keys, gain, kv_weight]
    body = functools.partial(tri_kernel, first_row=number * rows, rows=rows)
    aliases = {}
    if held is None:
        kernel = lambda *refs: body(*refs[:6], None, *refs[6:])
    else:
        kernel = body
        in_specs.append(pl.BlockSpec(memory_space=pl.ANY))
        args.append(held)
        aliases = {6: 0}
    return pl.pallas_call(
        kernel,
        grid=(1,),
        in_specs=in_specs,
        out_specs=[
            pl.BlockSpec((rows, width), lambda i: (number, 0)),
            whole((rows, 2 * DIM)),
        ],
        out_shape=[
            jax.ShapeDtypeStruct((token_rows, width), jnp.bfloat16),
            jax.ShapeDtypeStruct((rows, 2 * DIM), jnp.bfloat16),
        ],
        scratch_shapes=[
            pltpu.VMEM((W2, rows, DIM), jnp.bfloat16),
            pltpu.VMEM((W2, rows, DIM), jnp.float32),
            pltpu.VMEM((1, rows, DIM), jnp.bfloat16),
            pltpu.VMEM((W2, rows, DIM), jnp.bfloat16),
            pltpu.VMEM((W2, rows, DIM), jnp.float32),
            pltpu.VMEM((rows, width), jnp.bfloat16),
            pltpu.VMEM((W1 + 16, 2 * DIM), jnp.float32),
        ],
        input_output_aliases=aliases,
        compiler_params=pltpu.CompilerParams(vmem_limit_bytes=40 * 1024 * 1024),
        cost_estimate=pl.CostEstimate(
            flops=4 * rows * HEADS * W2 * 256 * DIM, bytes_accessed=2 << 20, transcendentals=0
        ),
        name="tri_part",
    )(*args)


def att_kernel(me_ref, q_ref, far_ref, own_ref, out_ref, q_scr, k_scr, v_scr, s_scr, top_scr, total_scr, acc_scr, *, rows, step, group):
    me = me_ref[0]
    far = far_ref.shape[0]
    tokens = k_scr.shape[0]
    k_scr[:far, :] = far_ref[:, :DIM]
    v_scr[:far, :] = far_ref[:, DIM:]
    if far < tokens:
        k_scr[far:, :] = jnp.zeros((tokens - far, DIM), jnp.bfloat16)
        v_scr[far:, :] = jnp.zeros((tokens - far, DIM), jnp.bfloat16)
    here = pl.ds(pl.multiple_of(me * rows, rows), rows)
    k_scr[here, :] = own_ref[:, :DIM]
    v_scr[here, :] = own_ref[:, DIM:]
    full = (me * rows) // step
    size = group * rows

    def one_group(g, _):
        for h in range(group):
            lanes = pl.ds(pl.multiple_of((g * group + h) * DIM, DIM), DIM)
            q_scr[h * rows : (h + 1) * rows, :] = q_ref[:, lanes]
        top_scr[...] = jnp.full((size, DIM), NEG, jnp.float32)

        def scores(b):
            keys = k_scr[pl.ds(pl.multiple_of(b * step, step), step), :]
            return lax.dot_general(q_scr[...], keys, NT, preferred_element_type=jnp.float32)

        def keep(b, score):
            s_scr[b] = score
            top = top_scr[...]
            for c in range(step // DIM):
                top = jnp.maximum(top, score[:, c * DIM : (c + 1) * DIM])
            top_scr[...] = top

        def first_pass(b, _):
            keep(b, scores(b))
            return 0

        lax.fori_loop(0, full, first_pass, 0)
        key_pos = full * step + lax.broadcasted_iota(jnp.int32, (rows, step), 1)
        query_pos = me * rows + lax.broadcasted_iota(jnp.int32, (rows, step), 0)
        last = scores(full).reshape(group, rows, step)
        last = jnp.where((key_pos <= query_pos)[None], last, NEG).reshape(size, step)
        keep(full, last)
        top = jnp.max(top_scr[...], axis=-1, keepdims=True)
        top_scr[...] = jnp.broadcast_to(top, (size, DIM))
        total_scr[...] = jnp.zeros((size, DIM), jnp.float32)
        acc_scr[...] = jnp.zeros((size, DIM), jnp.float32)

        def second_pass(b, _):
            values = v_scr[pl.ds(pl.multiple_of(b * step, step), step), :]
            top = top_scr[...]
            weights = []
            total = total_scr[...]
            for c in range(step // DIM):
                weight = jnp.exp2((s_scr[b, :, c * DIM : (c + 1) * DIM] - top) * EXP2_SCALE)
                total = total + weight
                weights.append(weight.astype(jnp.bfloat16))
            total_scr[...] = total
            acc_scr[...] += jnp.dot(
                jnp.concatenate(weights, -1), values, preferred_element_type=jnp.float32
            )
            return 0

        lax.fori_loop(0, full + 1, second_pass, 0)
        result = acc_scr[...] / jnp.sum(total_scr[...], axis=-1, keepdims=True)
        result = result.astype(jnp.bfloat16)
        for h in range(group):
            lanes = pl.ds(pl.multiple_of((g * group + h) * DIM, DIM), DIM)
            out_ref[:, lanes] = result[h * rows : (h + 1) * rows, :]
        return 0

    lax.fori_loop(0, HEADS // group, one_group, 0)


def att_call(me, att_query, far, own, step=256, group=4):
    rows, width = att_query.shape
    tokens = 16 * rows
    size = group * rows
    whole = lambda shape: pl.BlockSpec(shape, lambda i: (0,) * len(shape))
    return pl.pallas_call(
        functools.partial(att_kernel, rows=rows, step=step, group=group),
        grid=(1,),
        in_specs=[
            pl.BlockSpec(memory_space=pltpu.SMEM),
            whole(att_query.shape),
            whole(far.shape),
            whole(own.shape),
        ],
        out_specs=whole(att_query.shape),
        out_shape=jax.ShapeDtypeStruct(att_query.shape, jnp.bfloat16),
        scratch_shapes=[
            pltpu.VMEM((size, DIM), jnp.bfloat16),
            pltpu.VMEM((tokens, DIM), jnp.bfloat16),
            pltpu.VMEM((tokens, DIM), jnp.bfloat16),
            pltpu.VMEM((tokens // step, size, step), jnp.float32),
            pltpu.VMEM((size, DIM), jnp.float32),
            pltpu.VMEM((size, DIM), jnp.float32),
            pltpu.VMEM((size, DIM), jnp.float32),
        ],
        compiler_params=pltpu.CompilerParams(vmem_limit_bytes=48 * 1024 * 1024),
        cost_estimate=pl.CostEstimate(
            flops=4 * rows * HEADS * tokens * DIM, bytes_accessed=3 << 20, transcendentals=0
        ),
        name="causal",
    )(me, att_query, far, own)


def passed_along(block, axis):
    count = lax.axis_size(axis)
    return lax.ppermute(block, axis, [(i, i + 1) for i in range(count - 1)])


def per_device(tri_query, tri_keys, att_query, norm_gain, kv_weight):
    rows = tri_query.shape[0]
    half = rows // 2
    shards = lax.axis_size("seq")
    me = lax.axis_index("seq")
    place = jnp.reshape(me, (1,)).astype(jnp.int32)
    gain = norm_gain.reshape(1, -1)
    behind = passed_along(tri_keys, "seq")
    held, kv_late = tri_call(place, tri_query, behind, tri_keys, gain, kv_weight, None, 1, half)
    before = passed_along(kv_late[half - shards :], "seq")
    tri_out, kv_early = tri_call(place, tri_query, behind, tri_keys, gain, kv_weight, held, 0, half)
    own = jnp.concatenate([kv_early, kv_late], 0)
    share = lax.dynamic_slice_in_dim(jnp.concatenate([before, own], 0), shards - me, rows - 1, 0)
    far = lax.all_gather(share, "seq", axis=0, tiled=True)
    attended = att_call(place, att_query, far, own)
    return (tri_out, attended)


def solution(mesh):
    in_specs = (P(("dp", "seq"), None), P(("dp", "seq"), None), P(("dp", "seq"), None), P(), P())
    out_specs = (P(("dp", "seq"), None), P(("dp", "seq"), None))
    return jax.shard_map(
        per_device, mesh=mesh, in_specs=in_specs, out_specs=out_specs, check_vma=False
    )
```

```python
import functools

import jax
import jax.numpy as jnp
from jax import lax
from jax.experimental import pallas as pl
from jax.experimental.pallas import tpu as pltpu
from jax.sharding import PartitionSpec as P

HEADS = 16
DIM = 128
W1 = 128
W2 = 16
NEG = -1e30
SCALE = DIM**-0.5
EXP2_SCALE = SCALE * 1.4426950408889634
PIECE = 16
BLOCK = 16
NT = (((1,), (1,)), ((), ()))


def tri_kernel(
    me_ref, q_ref, prev_ref, cur_ref, gain_ref, weight_ref, held_ref, out_ref, kv_ref,
    k2_scr, v2_scr, mask_scr, s_scr, top_scr, square_scr, shift_scr, *, first_row, rows,
):
    first_shard = me_ref[0] == 0

    shift_scr[0:16, :] = prev_ref[W1 - 16 : W1, 2 * DIM :].astype(jnp.float32)
    shift_scr[16:, :] = cur_ref[:, 2 * DIM :].astype(jnp.float32)
    for lag in range(W2):
        at = 16 + first_row - lag
        k2_scr[lag] = shift_scr[at : at + rows, :DIM].astype(jnp.bfloat16)
        v2_scr[lag] = shift_scr[at : at + rows, DIM:]
    row = first_row + lax.broadcasted_iota(jnp.int32, (rows, DIM), 0)
    col = lax.broadcasted_iota(jnp.int32, (rows, DIM), 1)
    own = col <= row
    mask_scr[0] = jnp.where(own, 1.0, 0.0).astype(jnp.bfloat16)
    k1 = jnp.concatenate([cur_ref[:, :DIM], prev_ref[:, :DIM]], 0)
    v1 = jnp.concatenate([cur_ref[:, DIM : 2 * DIM], prev_ref[:, DIM : 2 * DIM]], 0)

    blocks = [slice(at, at + BLOCK) for at in range(0, rows, BLOCK)]
    pieces = [slice(at, at + PIECE) for at in range(0, W2, PIECE)]

    def lanes_of(head):
        return pl.ds(pl.multiple_of(head * DIM, DIM), DIM)

    def score_step(query, block, lags, slot, top, first):
        mq = jnp.concatenate([query * k2_scr[lag, block] for lag in range(lags.start, lags.stop)], 0)
        both = lax.dot_general(mq, k1, NT, preferred_element_type=jnp.float32)
        row = first_row + block.start + lax.broadcasted_iota(jnp.int32, (BLOCK, DIM), 0)
        own = lax.broadcasted_iota(jnp.int32, (BLOCK, DIM), 1) <= row
        for n, lag in enumerate(range(lags.start, lags.stop)):
            here = both[n * BLOCK : (n + 1) * BLOCK]
            if first:
                allowed = own
                if first_row + block.start < lag:
                    allowed = own & (lag <= row)
                score = jnp.where(allowed, here[:, :DIM], NEG)
            else:
                score = jnp.where(own, here[:, :DIM], here[:, DIM:])
            s_scr[slot, lag, block] = score
            top = score if top is None else jnp.maximum(top, score)
        return top

    def weigh_step(block, lags, slot, top, total, acc):
        halves = []
        mask = mask_scr[0, block]
        for lag in range(lags.start, lags.stop):
            weight = jnp.exp2((s_scr[slot, lag, block] - top) * EXP2_SCALE)
            total = weight if total is None else total + weight
            rounded = weight.astype(jnp.bfloat16)
            w_own = rounded * mask
            halves.append(jnp.concatenate([w_own, rounded - w_own], -1))
        paired = jnp.dot(jnp.concatenate(halves, 0), v1, preferred_element_type=jnp.float32)
        for n, lag in enumerate(range(lags.start, lags.stop)):
            part = paired[n * BLOCK : (n + 1) * BLOCK] * v2_scr[lag, block]
            acc = part if acc is None else acc + part
        return total, acc

    def spread(top):
        return jnp.broadcast_to(jnp.max(top, axis=-1, keepdims=True), top.shape)

    def both_steps(score_head, score_slot, weigh_head, first):
        for block in blocks:
            query = q_ref[block, lanes_of(score_head)]
            next_top = total = acc = None
            top = top_scr[1 - score_slot, block]
            for lags in pieces:
                next_top = score_step(query, block, lags, score_slot, next_top, first)
                total, acc = weigh_step(block, lags, 1 - score_slot, top, total, acc)
            top_scr[score_slot, block] = spread(next_top)
            result = (acc / jnp.sum(total, axis=-1, keepdims=True)).astype(jnp.bfloat16)
            out_ref[block, lanes_of(weigh_head)] = result
            wide = result.astype(jnp.float32)
            square_scr[block] += wide * wide

    def all_heads(first):
        square_scr[...] = jnp.zeros((rows, DIM), jnp.float32)
        for block in blocks:
            top = None
            for lags in pieces:
                top = score_step(q_ref[block, lanes_of(0)], block, lags, 0, top, first)
            top_scr[0, block] = spread(top)

        def pair(k, carried):
            both_steps(2 * k + 1, 1, 2 * k, first)
            both_steps(jnp.minimum(2 * k + 2, HEADS - 1), 0, 2 * k + 1, first)
            return carried

        lax.fori_loop(0, HEADS // 2, pair, 0)
        return square_scr[...]

    def finish(square):
        mean = jnp.sum(square, axis=-1, keepdims=True) * (1.0 / (HEADS * DIM))
        inverse = lax.rsqrt(mean + 1e-6)
        normed = (out_ref[...].astype(jnp.float32) * inverse * gain_ref[...]).astype(jnp.bfloat16)
        kv_ref[...] = jnp.dot(
            normed, weight_ref[...], preferred_element_type=jnp.float32
        ).astype(jnp.bfloat16)

    @pl.when(first_shard)
    def _():
        finish(all_heads(True))

    @pl.when(jnp.logical_not(first_shard))
    def _():
        finish(all_heads(False))


def tri_call(me, tri_query, behind, tri_keys, gain, kv_weight, held, number, rows):
    token_rows, width = tri_query.shape
    whole = lambda shape: pl.BlockSpec(shape, lambda i: (0,) * len(shape))
    in_specs = [
        pl.BlockSpec(memory_space=pltpu.SMEM),
        pl.BlockSpec((rows, width), lambda i: (number, 0)),
        whole(behind.shape),
        whole(tri_keys.shape),
        whole(gain.shape),
        whole(kv_weight.shape),
    ]
    args = [me, tri_query, behind, tri_keys, gain, kv_weight]
    body = functools.partial(tri_kernel, first_row=number * rows, rows=rows)
    aliases = {}
    if held is None:
        kernel = lambda *refs: body(*refs[:6], None, *refs[6:])
    else:
        kernel = body
        in_specs.append(pl.BlockSpec(memory_space=pl.ANY))
        args.append(held)
        aliases = {6: 0}
    return pl.pallas_call(
        kernel,
        grid=(1,),
        in_specs=in_specs,
        out_specs=[
            pl.BlockSpec((rows, width), lambda i: (number, 0)),
            whole((rows, 2 * DIM)),
        ],
        out_shape=[
            jax.ShapeDtypeStruct((token_rows, width), jnp.bfloat16),
            jax.ShapeDtypeStruct((rows, 2 * DIM), jnp.bfloat16),
        ],
        scratch_shapes=[
            pltpu.VMEM((W2, rows, DIM), jnp.bfloat16),
            pltpu.VMEM((W2, rows, DIM), jnp.float32),
            pltpu.VMEM((1, rows, DIM), jnp.bfloat16),
            pltpu.VMEM((2, W2, rows, DIM), jnp.float32),
            pltpu.VMEM((2, rows, DIM), jnp.float32),
            pltpu.VMEM((rows, DIM), jnp.float32),
            pltpu.VMEM((W1 + 16, 2 * DIM), jnp.float32),
        ],
        input_output_aliases=aliases,
        compiler_params=pltpu.CompilerParams(vmem_limit_bytes=40 * 1024 * 1024),
        cost_estimate=pl.CostEstimate(
            flops=4 * rows * HEADS * W2 * 256 * DIM, bytes_accessed=2 << 20, transcendentals=0
        ),
        name="tri_part",
    )(*args)


KEYS = 256


def att_kernel(me_ref, q_ref, far_ref, own_ref, out_ref, k_scr, v_scr, s_scr, top_scr, *, rows):
    me = me_ref[0]
    tokens = k_scr.shape[0]
    before = tokens - rows
    k_scr[:before, :] = far_ref[:before, :DIM]
    v_scr[:before, :] = far_ref[:before, DIM:]
    k_scr[before:, :] = own_ref[:, :DIM]
    v_scr[before:, :] = own_ref[:, DIM:]
    tiles = tokens // DIM
    caps = [jnp.where(tile < me, -NEG, NEG) for tile in range(tiles - 1)]

    def lanes_of(head):
        return pl.ds(pl.multiple_of(head * DIM, DIM), DIM)

    def score_step(query, slot, at, top):
        both = lax.dot_general(
            query, k_scr[at : at + KEYS, :], NT, preferred_element_type=jnp.float32
        )
        for n in range(KEYS // DIM):
            tile = at // DIM + n
            score = both[:, n * DIM : (n + 1) * DIM]
            if tile == tiles - 1:
                row = lax.broadcasted_iota(jnp.int32, (rows, DIM), 0)
                col = lax.broadcasted_iota(jnp.int32, (rows, DIM), 1)
                score = jnp.where(col <= row, score, NEG)
            else:
                score = jnp.minimum(score, caps[tile])
            s_scr[slot, tile] = score
            top = score if top is None else jnp.maximum(top, score)
        return top

    def weigh_step(slot, at, top, total, acc):
        weights = []
        for n in range(KEYS // DIM):
            weight = jnp.exp2((s_scr[slot, at // DIM + n] - top) * EXP2_SCALE)
            total = weight if total is None else total + weight
            weights.append(weight.astype(jnp.bfloat16))
        return total, (acc or []) + weights

    def settle(slot, top):
        top_scr[slot] = jnp.broadcast_to(jnp.max(top, axis=-1, keepdims=True), (rows, DIM))

    def both_steps(score_head, score_slot, weigh_head):
        query = q_ref[:, lanes_of(score_head)]
        next_top = total = acc = None
        top = top_scr[1 - score_slot]
        for at in range(0, tokens, KEYS):
            next_top = score_step(query, score_slot, at, next_top)
            total, acc = weigh_step(1 - score_slot, at, top, total, acc)
        settle(score_slot, next_top)
        acc = jnp.dot(jnp.concatenate(acc, -1), v_scr[...], preferred_element_type=jnp.float32)
        result = acc / jnp.sum(total, axis=-1, keepdims=True)
        out_ref[:, lanes_of(weigh_head)] = result.astype(jnp.bfloat16)

    top = None
    for at in range(0, tokens, KEYS):
        top = score_step(q_ref[:, lanes_of(0)], 0, at, top)
    settle(0, top)

    def pair(k, carried):
        both_steps(2 * k + 1, 1, 2 * k)
        both_steps(jnp.minimum(2 * k + 2, HEADS - 1), 0, 2 * k + 1)
        return carried

    lax.fori_loop(0, HEADS // 2, pair, 0)


def att_call(me, att_query, far, own):
    rows, width = att_query.shape
    tokens = 16 * rows
    whole = lambda shape: pl.BlockSpec(shape, lambda i: (0,) * len(shape))
    return pl.pallas_call(
        functools.partial(att_kernel, rows=rows),
        grid=(1,),
        in_specs=[
            pl.BlockSpec(memory_space=pltpu.SMEM),
            whole(att_query.shape),
            whole(far.shape),
            whole(own.shape),
        ],
        out_specs=whole(att_query.shape),
        out_shape=jax.ShapeDtypeStruct(att_query.shape, jnp.bfloat16),
        scratch_shapes=[
            pltpu.VMEM((tokens, DIM), jnp.bfloat16),
            pltpu.VMEM((tokens, DIM), jnp.bfloat16),
            pltpu.VMEM((2, tokens // DIM, rows, DIM), jnp.float32),
            pltpu.VMEM((2, rows, DIM), jnp.float32),
        ],
        compiler_params=pltpu.CompilerParams(vmem_limit_bytes=48 * 1024 * 1024),
        cost_estimate=pl.CostEstimate(
            flops=4 * rows * HEADS * tokens * DIM, bytes_accessed=3 << 20, transcendentals=0
        ),
        name="causal",
    )(me, att_query, far, own)


def passed_along(block, axis):
    count = lax.axis_size(axis)
    return lax.ppermute(block, axis, [(i, i + 1) for i in range(count - 1)])


def per_device(tri_query, tri_keys, att_query, norm_gain, kv_weight):
    rows = tri_query.shape[0]
    half = rows // 2
    shards = lax.axis_size("seq")
    me = lax.axis_index("seq")
    place = jnp.reshape(me, (1,)).astype(jnp.int32)
    gain = norm_gain.reshape(1, -1)
    behind = passed_along(tri_keys, "seq")
    held, kv_late = tri_call(place, tri_query, behind, tri_keys, gain, kv_weight, None, 1, half)
    before = passed_along(kv_late[half - shards :], "seq")
    tri_out, kv_early = tri_call(place, tri_query, behind, tri_keys, gain, kv_weight, held, 0, half)
    own = jnp.concatenate([kv_early, kv_late], 0)
    share = lax.dynamic_slice_in_dim(jnp.concatenate([before, own], 0), shards - me, rows - 1, 0)
    far = lax.all_gather(share, "seq", axis=0, tiled=True)
    attended = att_call(place, att_query, far, own)
    return (tri_out, attended)


def solution(mesh):
    in_specs = (P(("dp", "seq"), None), P(("dp", "seq"), None), P(("dp", "seq"), None), P(), P())
    out_specs = (P(("dp", "seq"), None), P(("dp", "seq"), None))
    return jax.shard_map(
        per_device, mesh=mesh, in_specs=in_specs, out_specs=out_specs, check_vma=False
    )
```

```python
import functools

import jax
import jax.numpy as jnp
from jax import lax
from jax.experimental import pallas as pl
from jax.experimental.pallas import tpu as pltpu
from jax.sharding import PartitionSpec as P

HEADS = 16
DIM = 128
W1 = 128
W2 = 16
NEG = -1e30
SCALE = DIM**-0.5
EXP2_SCALE = SCALE * 1.4426950408889634
PIECE = 16
BLOCK = 16
NT = (((1,), (1,)), ((), ()))


def tri_kernel(
    me_ref, staged_ref, q_ref, prev_ref, cur_ref, gain_ref, weight_ref, held_ref, out_ref, kv_ref,
    k2_scr, v2_scr, mask_scr, s_scr, top_scr, square_scr, shift_scr, *, first_row, rows,
):
    first_shard = me_ref[0] == 0

    shift_scr[0:16, :] = prev_ref[W1 - 16 : W1, 2 * DIM :].astype(jnp.float32)
    shift_scr[16:, :] = cur_ref[:, 2 * DIM :].astype(jnp.float32)
    for lag in range(W2):
        at = 16 + first_row - lag
        k2_scr[lag] = shift_scr[at : at + rows, :DIM].astype(jnp.bfloat16)
        v2_scr[lag] = shift_scr[at : at + rows, DIM:]
    row = first_row + lax.broadcasted_iota(jnp.int32, (rows, DIM), 0)
    col = lax.broadcasted_iota(jnp.int32, (rows, DIM), 1)
    own = col <= row
    mask_scr[0] = jnp.where(own, 1.0, 0.0).astype(jnp.bfloat16)
    k1 = jnp.concatenate([cur_ref[:, :DIM], prev_ref[:, :DIM]], 0)
    v1 = jnp.concatenate([cur_ref[:, DIM : 2 * DIM], prev_ref[:, DIM : 2 * DIM]], 0)

    blocks = [slice(at, at + BLOCK) for at in range(0, rows, BLOCK)]
    pieces = [slice(at, at + PIECE) for at in range(0, W2, PIECE)]

    def lanes_of(head):
        return pl.ds(pl.multiple_of(head * DIM, DIM), DIM)

    def score_step(query, block, lags, slot, top, first):
        mq = jnp.concatenate([query * k2_scr[lag, block] for lag in range(lags.start, lags.stop)], 0)
        both = lax.dot_general(mq, k1, NT, preferred_element_type=jnp.float32)
        row = first_row + block.start + lax.broadcasted_iota(jnp.int32, (BLOCK, DIM), 0)
        own = lax.broadcasted_iota(jnp.int32, (BLOCK, DIM), 1) <= row
        for n, lag in enumerate(range(lags.start, lags.stop)):
            here = both[n * BLOCK : (n + 1) * BLOCK]
            if first:
                allowed = own
                if first_row + block.start < lag:
                    allowed = own & (lag <= row)
                score = jnp.where(allowed, here[:, :DIM], NEG)
            else:
                score = jnp.where(own, here[:, :DIM], here[:, DIM:])
            s_scr[slot, lag, block] = score
            top = score if top is None else jnp.maximum(top, score)
        return top

    def weigh_step(block, lags, slot, top, total, acc):
        halves = []
        mask = mask_scr[0, block]
        for lag in range(lags.start, lags.stop):
            weight = jnp.exp2((s_scr[slot, lag, block] - top) * EXP2_SCALE)
            total = weight if total is None else total + weight
            rounded = weight.astype(jnp.bfloat16)
            w_own = rounded * mask
            halves.append(jnp.concatenate([w_own, rounded - w_own], -1))
        paired = jnp.dot(jnp.concatenate(halves, 0), v1, preferred_element_type=jnp.float32)
        for n, lag in enumerate(range(lags.start, lags.stop)):
            part = paired[n * BLOCK : (n + 1) * BLOCK] * v2_scr[lag, block]
            acc = part if acc is None else acc + part
        return total, acc

    def spread(top):
        return jnp.broadcast_to(jnp.max(top, axis=-1, keepdims=True), top.shape)

    def both_steps(score_head, score_slot, weigh_head, first):
        for block in blocks:
            query = q_ref[block, lanes_of(score_head)]
            next_top = total = acc = None
            top = top_scr[1 - score_slot, block]
            for lags in pieces:
                next_top = score_step(query, block, lags, score_slot, next_top, first)
                total, acc = weigh_step(block, lags, 1 - score_slot, top, total, acc)
            top_scr[score_slot, block] = spread(next_top)
            result = (acc / jnp.sum(total, axis=-1, keepdims=True)).astype(jnp.bfloat16)
            out_ref[block, lanes_of(weigh_head)] = result
            wide = result.astype(jnp.float32)
            square_scr[block] += wide * wide

    def all_heads(first):
        square_scr[...] = jnp.zeros((rows, DIM), jnp.float32)
        for block in blocks:
            top = None
            for lags in pieces:
                top = score_step(q_ref[block, lanes_of(0)], block, lags, 0, top, first)
            top_scr[0, block] = spread(top)

        def pair(k, carried):
            both_steps(2 * k + 1, 1, 2 * k, first)
            both_steps(jnp.minimum(2 * k + 2, HEADS - 1), 0, 2 * k + 1, first)
            return carried

        lax.fori_loop(0, HEADS // 2, pair, 0)
        return square_scr[...]

    def finish(square):
        mean = jnp.sum(square, axis=-1, keepdims=True) * (1.0 / (HEADS * DIM))
        inverse = lax.rsqrt(mean + 1e-6)
        normed = (out_ref[...].astype(jnp.float32) * inverse * gain_ref[...]).astype(jnp.bfloat16)
        kv_ref[...] = jnp.dot(
            normed, weight_ref[...], preferred_element_type=jnp.float32
        ).astype(jnp.bfloat16)

    @pl.when(first_shard)
    def _():
        finish(all_heads(True))

    @pl.when(jnp.logical_not(first_shard))
    def _():
        finish(all_heads(False))


def tri_call(me, staged, tri_query, behind, tri_keys, gain, kv_weight, held, number, rows):
    token_rows, width = tri_query.shape
    whole = lambda shape: pl.BlockSpec(shape, lambda i: (0,) * len(shape))
    in_specs = [
        pl.BlockSpec(memory_space=pltpu.SMEM),
        pl.BlockSpec(memory_space=pl.ANY),
        pl.BlockSpec((rows, width), lambda i: (number, 0)),
        whole(behind.shape),
        whole(tri_keys.shape),
        whole(gain.shape),
        whole(kv_weight.shape),
    ]
    args = [me, staged, tri_query, behind, tri_keys, gain, kv_weight]
    body = functools.partial(tri_kernel, first_row=number * rows, rows=rows)
    aliases = {}
    if held is None:
        kernel = lambda *refs: body(*refs[:7], None, *refs[7:])
    else:
        kernel = body
        in_specs.append(pl.BlockSpec(memory_space=pl.ANY))
        args.append(held)
        aliases = {7: 0}
    return pl.pallas_call(
        kernel,
        grid=(1,),
        in_specs=in_specs,
        out_specs=[
            pl.BlockSpec((rows, width), lambda i: (number, 0)),
            whole((rows, 2 * DIM)),
        ],
        out_shape=[
            jax.ShapeDtypeStruct((token_rows, width), jnp.bfloat16),
            jax.ShapeDtypeStruct((rows, 2 * DIM), jnp.bfloat16),
        ],
        scratch_shapes=[
            pltpu.VMEM((W2, rows, DIM), jnp.bfloat16),
            pltpu.VMEM((W2, rows, DIM), jnp.float32),
            pltpu.VMEM((1, rows, DIM), jnp.bfloat16),
            pltpu.VMEM((2, W2, rows, DIM), jnp.float32),
            pltpu.VMEM((2, rows, DIM), jnp.float32),
            pltpu.VMEM((rows, DIM), jnp.float32),
            pltpu.VMEM((W1 + 16, 2 * DIM), jnp.float32),
        ],
        input_output_aliases=aliases,
        compiler_params=pltpu.CompilerParams(vmem_limit_bytes=40 * 1024 * 1024),
        cost_estimate=pl.CostEstimate(
            flops=4 * rows * HEADS * W2 * 256 * DIM, bytes_accessed=2 << 20, transcendentals=0
        ),
        name="tri_part",
    )(*args)


def stage_kernel(*refs):
    out_ref = refs[-1]
    total = jnp.zeros(out_ref.shape, jnp.float32)
    for ref in refs[:-1]:
        total += ref[0:1, 0:DIM].astype(jnp.float32)
    out_ref[...] = total


def stage_call(*arrays):
    return pl.pallas_call(
        stage_kernel,
        grid=(1,),
        in_specs=[pl.BlockSpec(a.shape, lambda i: (0, 0)) for a in arrays],
        out_specs=pl.BlockSpec((8, DIM), lambda i: (0, 0)),
        out_shape=jax.ShapeDtypeStruct((8, DIM), jnp.float32),
        compiler_params=pltpu.CompilerParams(vmem_limit_bytes=8 * 1024 * 1024),
        cost_estimate=pl.CostEstimate(flops=0, bytes_accessed=3 << 20, transcendentals=0),
        name="stage",
    )(*arrays)


SPAN = 2


def att_kernel(me_ref, q_ref, far_ref, own_ref, out_ref, s_scr, top_scr, *, rows):
    me = me_ref[0]
    shards = far_ref.shape[0] // rows + 1

    def lanes_of(head):
        return pl.ds(pl.multiple_of(head * DIM, DIM), DIM)

    def attend(before):
        tiles = before + 1
        caps = [jnp.where(tile < me, -NEG, NEG) for tile in range(before)]

        def of_tile(tile, lanes):
            if tile == before:
                return own_ref[:, lanes]
            return far_ref[tile * DIM : (tile + 1) * DIM, lanes]

        def score_step(query, slot, tile, top):
            keys = [of_tile(tile, slice(0, DIM)), of_tile(tile + 1, slice(0, DIM))]
            both = lax.dot_general(
                query, jnp.concatenate(keys, 0), NT, preferred_element_type=jnp.float32
            )
            for n in range(2):
                score = both[:, n * DIM : (n + 1) * DIM]
                if tile + n == before:
                    row = lax.broadcasted_iota(jnp.int32, (rows, DIM), 0)
                    col = lax.broadcasted_iota(jnp.int32, (rows, DIM), 1)
                    score = jnp.where(col <= row, score, NEG)
                else:
                    score = jnp.minimum(score, caps[tile + n])
                s_scr[slot, tile + n] = score
                top = score if top is None else jnp.maximum(top, score)
            return top

        def weigh_step(slot, tile, top, total, weights):
            for n in range(2):
                weight = jnp.exp2((s_scr[slot, tile + n] - top) * EXP2_SCALE)
                total = weight if total is None else total + weight
                weights.append(weight.astype(jnp.bfloat16))
            return total

        def settle(slot, top):
            top_scr[slot] = jnp.broadcast_to(jnp.max(top, axis=-1, keepdims=True), (rows, DIM))

        def both_steps(score_head, score_slot, weigh_head):
            query = q_ref[:, lanes_of(score_head)]
            next_top = total = None
            weights = []
            top = top_scr[1 - score_slot]
            for tile in range(0, tiles, 2):
                next_top = score_step(query, score_slot, tile, next_top)
                total = weigh_step(1 - score_slot, tile, top, total, weights)
            settle(score_slot, next_top)
            values = jnp.concatenate([of_tile(t, slice(DIM, 2 * DIM)) for t in range(tiles)], 0)
            acc = jnp.dot(
                jnp.concatenate(weights, -1), values, preferred_element_type=jnp.float32
            )
            result = acc / jnp.sum(total, axis=-1, keepdims=True)
            out_ref[:, lanes_of(weigh_head)] = result.astype(jnp.bfloat16)

        top = None
        for tile in range(0, tiles, 2):
            top = score_step(q_ref[:, lanes_of(0)], 0, tile, top)
        settle(0, top)

        def pair(k, carried):
            both_steps(2 * k + 1, 1, 2 * k)
            both_steps(jnp.minimum(2 * k + 2, HEADS - 1), 0, 2 * k + 1)
            return carried

        lax.fori_loop(0, HEADS // 2, pair, 0)

    lowest = 0
    for before in range(1, shards + 1, SPAN):
        chosen = (me >= lowest) & (me <= before)
        pl.when(chosen)(functools.partial(attend, before))
        lowest = before + 1


def att_call(me, att_query, far, own):
    rows, width = att_query.shape
    tokens = 16 * rows
    whole = lambda shape: pl.BlockSpec(shape, lambda i: (0,) * len(shape))
    return pl.pallas_call(
        functools.partial(att_kernel, rows=rows),
        grid=(1,),
        in_specs=[
            pl.BlockSpec(memory_space=pltpu.SMEM),
            whole(att_query.shape),
            whole(far.shape),
            whole(own.shape),
        ],
        out_specs=whole(att_query.shape),
        out_shape=jax.ShapeDtypeStruct(att_query.shape, jnp.bfloat16),
        scratch_shapes=[
            pltpu.VMEM((2, tokens // DIM, rows, DIM), jnp.float32),
            pltpu.VMEM((2, rows, DIM), jnp.float32),
        ],
        compiler_params=pltpu.CompilerParams(vmem_limit_bytes=48 * 1024 * 1024),
        cost_estimate=pl.CostEstimate(
            flops=4 * rows * HEADS * tokens * DIM, bytes_accessed=3 << 20, transcendentals=0
        ),
        name="causal",
    )(me, att_query, far, own)


def passed_along(block, axis):
    count = lax.axis_size(axis)
    return lax.ppermute(block, axis, [(i, i + 1) for i in range(count - 1)])


def per_device(tri_query, tri_keys, att_query, norm_gain, kv_weight):
    rows = tri_query.shape[0]
    half = rows // 2
    shards = lax.axis_size("seq")
    me = lax.axis_index("seq")
    place = jnp.reshape(me, (1,)).astype(jnp.int32)
    gain = norm_gain.reshape(1, -1)
    behind = passed_along(tri_keys, "seq")
    staged = stage_call(tri_query, tri_keys, kv_weight)
    held, kv_late = tri_call(place, staged, tri_query, behind, tri_keys, gain, kv_weight, None, 1, half)
    before = passed_along(kv_late[half - shards :], "seq")
    tri_out, kv_early = tri_call(place, staged, tri_query, behind, tri_keys, gain, kv_weight, held, 0, half)
    own = jnp.concatenate([kv_early, kv_late], 0)
    share = lax.dynamic_slice_in_dim(jnp.concatenate([before, own], 0), shards - me, rows - 1, 0)
    far = lax.all_gather(share, "seq", axis=0, tiled=True)
    attended = att_call(place, att_query, far, own)
    return (tri_out, attended)


def solution(mesh):
    in_specs = (P(("dp", "seq"), None), P(("dp", "seq"), None), P(("dp", "seq"), None), P(), P())
    out_specs = (P(("dp", "seq"), None), P(("dp", "seq"), None))
    return jax.shard_map(
        per_device, mesh=mesh, in_specs=in_specs, out_specs=out_specs, check_vma=False
    )
```

```python
import functools

import jax
import jax.numpy as jnp
from jax import lax
from jax.experimental import pallas as pl
from jax.experimental.pallas import tpu as pltpu
from jax.sharding import PartitionSpec as P

HEADS = 16
DIM = 128
W1 = 128
W2 = 16
NEG = -1e30
SCALE = DIM**-0.5
EXP2_SCALE = SCALE * 1.4426950408889634
NT = (((1,), (1,)), ((), ()))


def tri_kernel(
    me_ref, staged_ref, q_ref, prev_ref, cur_ref, gain_ref, weight_ref, held_ref, out_ref, kv_ref,
    wide_scr, q_scr, k2_scr, v2_scr, rest_scr, s_scr, *, first_row, rows,
):
    half = rows // 2
    first_shard = me_ref[0] == 0
    starts = (first_row, first_row + half)
    sides = (slice(0, DIM), slice(DIM, 2 * DIM))

    for head in range(HEADS):
        wide_scr[pl.ds(head, rows, stride=HEADS), :] = q_ref[
            :, head * DIM : (head + 1) * DIM
        ].astype(jnp.float32)
    q_scr[...] = wide_scr[...].astype(jnp.bfloat16).reshape(rows, HEADS, DIM)
    if first_row == 0:
        seconds = [prev_ref[W1 - W2 :, 2 * DIM :], cur_ref[:rows, 2 * DIM :]]
    else:
        seconds = [cur_ref[first_row - W2 : first_row + rows, 2 * DIM :]]
    seconds = jnp.concatenate(seconds, 0).astype(jnp.float32)
    for at in range(0, rows + W2, 8):
        key_two = seconds[at : at + 8, :DIM]
        val_two = seconds[at : at + 8, DIM:]
        k2_scr[at : at + 8] = jnp.broadcast_to(key_two[:, None], (8, HEADS, DIM)).astype(
            jnp.bfloat16
        )
        v2_scr[at : at + 8] = jnp.broadcast_to(val_two[:, None], (8, 8, DIM))
    tile = 16
    tiles = W1 // tile
    for n, start in enumerate(starts):
        now = start // tile
        for slot in range(tiles - 1):
            source = (now + 1 + slot) % tiles
            held = cur_ref if source < now else prev_ref
            rest_scr[n, slot] = held[source * tile : (source + 1) * tile, : 2 * DIM]

    def ring_of(n, lanes, group, step):
        place = pl.multiple_of(starts[n] + group * tile, tile)
        passed = lax.broadcasted_iota(jnp.int32, (tile, DIM), 0) <= step
        own = cur_ref[pl.ds(place, tile), lanes].astype(jnp.float32)
        prev = prev_ref[pl.ds(place, tile), lanes].astype(jnp.float32)
        mixed = jnp.where(passed, own, prev).astype(jnp.bfloat16)
        whole = [rest_scr[n, slot, :, lanes] for slot in range(tiles - 1)]
        return jnp.concatenate(whole + [mixed], 0)

    def diagonal(lanes, group, step):
        zero = jnp.zeros((DIM, DIM), jnp.bfloat16)
        return jnp.concatenate(
            [
                jnp.concatenate([ring_of(0, lanes, group, step), zero], -1),
                jnp.concatenate([zero, ring_of(1, lanes, group, step)], -1),
            ],
            0,
        )

    def leave(lanes, group):
        for n, start in enumerate(starts):
            place = pl.multiple_of(start + group * tile, tile)
            rest_scr[n, group, :, lanes] = cur_ref[pl.ds(place, tile), lanes]

    def score_step(group, step, slot, first):
        local = group * tile + step
        mq = []
        for lag in range(W2):
            mq.append(
                jnp.concatenate(
                    [
                        q_scr[n * half + local] * k2_scr[n * half + local + W2 - lag]
                        for n in range(2)
                    ],
                    -1,
                )
            )
        score = lax.dot_general(
            jnp.concatenate(mq, 0), diagonal(sides[0], group, step), NT, preferred_element_type=jnp.float32
        ).reshape(W2, HEADS, 2 * DIM)
        if first:
            lag = lax.broadcasted_iota(jnp.int32, (W2, HEADS, DIM), 0)
            col = lax.broadcasted_iota(jnp.int32, (W2, HEADS, DIM), 2)
            parts = []
            for n in range(2):
                row = starts[n] + local
                seat = jnp.right_shift(col, 4)
                past = jnp.where(seat + 1 + starts[n] // tile >= tiles, 0, 1)
                past = jnp.where(seat < group, 0, past)
                past = jnp.where(seat == tiles - 1, (col & (tile - 1)) - step, past)
                allowed = (past <= 0) & (lag <= row)
                parts.append(jnp.where(allowed, score[:, :, sides[n]], NEG))
            score = jnp.concatenate(parts, -1)
        s_scr[slot] = score
        top = jnp.max(score, axis=0)
        return tuple(jnp.max(top[:, side], axis=-1, keepdims=True) for side in sides)

    def weigh_step(group, step, slot, tops):
        local = group * tile + step
        total = [None, None]
        weights = []
        for lag in range(W2):
            pair = []
            for n in range(2):
                weight = jnp.exp2((s_scr[slot, lag, :, sides[n]] - tops[n]) * EXP2_SCALE)
                total[n] = weight if lag == 0 else total[n] + weight
                pair.append(weight.astype(jnp.bfloat16))
            weights.append(jnp.concatenate(pair, -1))
        paired = jnp.dot(
            jnp.concatenate(weights, 0),
            diagonal(sides[1], group, step),
            preferred_element_type=jnp.float32,
        ).reshape(W2, 2, 8, 2 * DIM)
        for n in range(2):
            acc = None
            for lag in range(W2):
                part = paired[lag, :, :, sides[n]] * v2_scr[n * half + local + W2 - lag][None]
                acc = part if acc is None else acc + part
            result = acc.reshape(HEADS, DIM) / jnp.sum(total[n], axis=-1, keepdims=True)
            place = pl.multiple_of((n * half + local) * HEADS, HEADS)
            wide_scr[pl.ds(place, HEADS), :] = result

    def all_queries(first):
        groups = half // tile

        def one_group(group, tops):
            for step in range(tile):
                after = (group, step + 1)
                if step == tile - 1:
                    after = (jnp.minimum(group + 1, groups - 1), 0)
                    leave(sides[0], group)
                next_tops = score_step(*after, (step + 1) % 2, first)
                weigh_step(group, step, step % 2, tops)
                if step == tile - 1:
                    leave(sides[1], group)
                tops = next_tops
            return tops

        lax.fori_loop(0, groups, one_group, score_step(0, 0, 0, first))

    @pl.when(first_shard)
    def _():
        all_queries(True)

    @pl.when(jnp.logical_not(first_shard))
    def _():
        all_queries(False)

    square = jnp.zeros((rows, DIM), jnp.float32)
    for head in range(HEADS):
        result = wide_scr[pl.ds(head, rows, stride=HEADS), :].astype(jnp.bfloat16)
        out_ref[:, head * DIM : (head + 1) * DIM] = result
        wide = result.astype(jnp.float32)
        square += wide * wide
    mean = jnp.sum(square, axis=-1, keepdims=True) * (1.0 / (HEADS * DIM))
    inverse = lax.rsqrt(mean + 1e-6)
    normed = (out_ref[...].astype(jnp.float32) * inverse * gain_ref[...]).astype(jnp.bfloat16)
    kv_ref[...] = jnp.dot(
        normed, weight_ref[...], preferred_element_type=jnp.float32
    ).astype(jnp.bfloat16)


def tri_call(me, staged, tri_query, behind, tri_keys, gain, kv_weight, held, number, rows):
    token_rows, width = tri_query.shape
    whole = lambda shape: pl.BlockSpec(shape, lambda i: (0,) * len(shape))
    in_specs = [
        pl.BlockSpec(memory_space=pltpu.SMEM),
        pl.BlockSpec(memory_space=pl.ANY),
        pl.BlockSpec((rows, width), lambda i: (number, 0)),
        whole(behind.shape),
        whole(tri_keys.shape),
        whole(gain.shape),
        whole(kv_weight.shape),
    ]
    args = [me, staged, tri_query, behind, tri_keys, gain, kv_weight]
    body = functools.partial(tri_kernel, first_row=number * rows, rows=rows)
    aliases = {}
    if held is None:
        kernel = lambda *refs: body(*refs[:7], None, *refs[7:])
    else:
        kernel = body
        in_specs.append(pl.BlockSpec(memory_space=pl.ANY))
        args.append(held)
        aliases = {7: 0}
    return pl.pallas_call(
        kernel,
        grid=(1,),
        in_specs=in_specs,
        out_specs=[
            pl.BlockSpec((rows, width), lambda i: (number, 0)),
            whole((rows, 2 * DIM)),
        ],
        out_shape=[
            jax.ShapeDtypeStruct((token_rows, width), jnp.bfloat16),
            jax.ShapeDtypeStruct((rows, 2 * DIM), jnp.bfloat16),
        ],
        scratch_shapes=[
            pltpu.VMEM((rows * HEADS, DIM), jnp.float32),
            pltpu.VMEM((rows, HEADS, DIM), jnp.bfloat16),
            pltpu.VMEM((rows + W2, HEADS, DIM), jnp.bfloat16),
            pltpu.VMEM((rows + W2, 8, DIM), jnp.float32),
            pltpu.VMEM((2, W1 // 16 - 1, 16, 2 * DIM), jnp.bfloat16),
            pltpu.VMEM((2, W2, HEADS, 2 * DIM), jnp.float32),
        ],
        input_output_aliases=aliases,
        compiler_params=pltpu.CompilerParams(vmem_limit_bytes=40 * 1024 * 1024),
        cost_estimate=pl.CostEstimate(
            flops=4 * rows * HEADS * W2 * 256 * DIM, bytes_accessed=2 << 20, transcendentals=0
        ),
        name="tri_part",
    )(*args)


def stage_kernel(*refs):
    out_ref = refs[-1]
    total = jnp.zeros(out_ref.shape, jnp.float32)
    for ref in refs[:-1]:
        total += ref[0:1, 0:DIM].astype(jnp.float32)
    out_ref[...] = total


def stage_call(*arrays):
    return pl.pallas_call(
        stage_kernel,
        grid=(1,),
        in_specs=[pl.BlockSpec(a.shape, lambda i: (0, 0)) for a in arrays],
        out_specs=pl.BlockSpec((8, DIM), lambda i: (0, 0)),
        out_shape=jax.ShapeDtypeStruct((8, DIM), jnp.float32),
        compiler_params=pltpu.CompilerParams(vmem_limit_bytes=8 * 1024 * 1024),
        cost_estimate=pl.CostEstimate(flops=0, bytes_accessed=3 << 20, transcendentals=0),
        name="stage",
    )(*arrays)


SPAN = 2


def att_kernel(me_ref, q_ref, far_ref, own_ref, out_ref, s_scr, top_scr, *, rows):
    me = me_ref[0]
    shards = far_ref.shape[0] // rows + 1

    def lanes_of(head):
        return pl.ds(pl.multiple_of(head * DIM, DIM), DIM)

    def attend(before):
        tiles = before + 1
        caps = [jnp.where(tile < me, -NEG, NEG) for tile in range(before)]

        def of_tile(tile, lanes):
            if tile == before:
                return own_ref[:, lanes]
            return far_ref[tile * DIM : (tile + 1) * DIM, lanes]

        def score_step(query, slot, tile, top):
            keys = [of_tile(tile, slice(0, DIM)), of_tile(tile + 1, slice(0, DIM))]
            both = lax.dot_general(
                query, jnp.concatenate(keys, 0), NT, preferred_element_type=jnp.float32
            )
            for n in range(2):
                score = both[:, n * DIM : (n + 1) * DIM]
                if tile + n == before:
                    row = lax.broadcasted_iota(jnp.int32, (rows, DIM), 0)
                    col = lax.broadcasted_iota(jnp.int32, (rows, DIM), 1)
                    score = jnp.where(col <= row, score, NEG)
                else:
                    score = jnp.minimum(score, caps[tile + n])
                s_scr[slot, tile + n] = score
                top = score if top is None else jnp.maximum(top, score)
            return top

        def weigh_step(slot, tile, top, total, weights):
            for n in range(2):
                weight = jnp.exp2((s_scr[slot, tile + n] - top) * EXP2_SCALE)
                total = weight if total is None else total + weight
                weights.append(weight.astype(jnp.bfloat16))
            return total

        def settle(slot, top):
            top_scr[slot] = jnp.broadcast_to(jnp.max(top, axis=-1, keepdims=True), (rows, DIM))

        def both_steps(score_head, score_slot, weigh_head):
            query = q_ref[:, lanes_of(score_head)]
            next_top = total = None
            weights = []
            top = top_scr[1 - score_slot]
            for tile in range(0, tiles, 2):
                next_top = score_step(query, score_slot, tile, next_top)
                total = weigh_step(1 - score_slot, tile, top, total, weights)
            settle(score_slot, next_top)
            values = jnp.concatenate([of_tile(t, slice(DIM, 2 * DIM)) for t in range(tiles)], 0)
            acc = jnp.dot(
                jnp.concatenate(weights, -1), values, preferred_element_type=jnp.float32
            )
            result = acc / jnp.sum(total, axis=-1, keepdims=True)
            out_ref[:, lanes_of(weigh_head)] = result.astype(jnp.bfloat16)

        top = None
        for tile in range(0, tiles, 2):
            top = score_step(q_ref[:, lanes_of(0)], 0, tile, top)
        settle(0, top)

        def pair(k, carried):
            both_steps(2 * k + 1, 1, 2 * k)
            both_steps(jnp.minimum(2 * k + 2, HEADS - 1), 0, 2 * k + 1)
            return carried

        lax.fori_loop(0, HEADS // 2, pair, 0)

    lowest = 0
    for before in range(1, shards + 1, SPAN):
        chosen = (me >= lowest) & (me <= before)
        pl.when(chosen)(functools.partial(attend, before))
        lowest = before + 1


def att_call(me, att_query, far, own):
    rows, width = att_query.shape
    tokens = 16 * rows
    whole = lambda shape: pl.BlockSpec(shape, lambda i: (0,) * len(shape))
    return pl.pallas_call(
        functools.partial(att_kernel, rows=rows),
        grid=(1,),
        in_specs=[
            pl.BlockSpec(memory_space=pltpu.SMEM),
            whole(att_query.shape),
            whole(far.shape),
            whole(own.shape),
        ],
        out_specs=whole(att_query.shape),
        out_shape=jax.ShapeDtypeStruct(att_query.shape, jnp.bfloat16),
        scratch_shapes=[
            pltpu.VMEM((2, tokens // DIM, rows, DIM), jnp.float32),
            pltpu.VMEM((2, rows, DIM), jnp.float32),
        ],
        compiler_params=pltpu.CompilerParams(vmem_limit_bytes=48 * 1024 * 1024),
        cost_estimate=pl.CostEstimate(
            flops=4 * rows * HEADS * tokens * DIM, bytes_accessed=3 << 20, transcendentals=0
        ),
        name="causal",
    )(me, att_query, far, own)


def passed_along(block, axis):
    count = lax.axis_size(axis)
    return lax.ppermute(block, axis, [(i, i + 1) for i in range(count - 1)])


def per_device(tri_query, tri_keys, att_query, norm_gain, kv_weight):
    rows = tri_query.shape[0]
    half = rows // 2
    shards = lax.axis_size("seq")
    me = lax.axis_index("seq")
    place = jnp.reshape(me, (1,)).astype(jnp.int32)
    gain = norm_gain.reshape(1, -1)
    behind = passed_along(tri_keys, "seq")
    staged = stage_call(tri_query, tri_keys, kv_weight)
    held, kv_late = tri_call(place, staged, tri_query, behind, tri_keys, gain, kv_weight, None, 1, half)
    before = passed_along(kv_late[half - shards :], "seq")
    tri_out, kv_early = tri_call(place, staged, tri_query, behind, tri_keys, gain, kv_weight, held, 0, half)
    own = jnp.concatenate([kv_early, kv_late], 0)
    share = lax.dynamic_slice_in_dim(jnp.concatenate([before, own], 0), shards - me, rows - 1, 0)
    far = lax.all_gather(share, "seq", axis=0, tiled=True)
    attended = att_call(place, att_query, far, own)
    return (tri_out, attended)


def solution(mesh):
    in_specs = (P(("dp", "seq"), None), P(("dp", "seq"), None), P(("dp", "seq"), None), P(), P())
    out_specs = (P(("dp", "seq"), None), P(("dp", "seq"), None))
    return jax.shard_map(
        per_device, mesh=mesh, in_specs=in_specs, out_specs=out_specs, check_vma=False
    )
```

```python
import functools

import jax
import jax.numpy as jnp
from jax import lax
from jax.experimental import pallas as pl
from jax.experimental.pallas import tpu as pltpu
from jax.sharding import PartitionSpec as P

HEADS = 16
DIM = 128
W1 = 128
W2 = 16
NEG = -1e30
SCALE = DIM**-0.5
EXP2_SCALE = SCALE * 1.4426950408889634
NT = (((1,), (1,)), ((), ()))


def tri_kernel(
    me_ref, staged_ref, q_ref, prev_ref, cur_ref, gain_ref, weight_ref, held_ref, out_ref, kv_ref,
    wide_scr, q_scr, k2_scr, v2_scr, rest_scr, s_scr, *, first_row, rows,
):
    half = rows // 2
    first_shard = me_ref[0] == 0
    starts = (first_row, first_row + half)
    sides = (slice(0, DIM), slice(DIM, 2 * DIM))

    for head in range(HEADS):
        wide_scr[pl.ds(head, rows, stride=HEADS), :] = q_ref[
            :, head * DIM : (head + 1) * DIM
        ].astype(jnp.float32)
    q_scr[...] = wide_scr[...].astype(jnp.bfloat16).reshape(rows, HEADS, DIM)
    if first_row == 0:
        seconds = [prev_ref[W1 - W2 :, 2 * DIM :], cur_ref[:rows, 2 * DIM :]]
    else:
        seconds = [cur_ref[first_row - W2 : first_row + rows, 2 * DIM :]]
    seconds = jnp.concatenate(seconds, 0).astype(jnp.float32)
    for at in range(0, rows + W2, 8):
        key_two = seconds[at : at + 8, :DIM]
        val_two = seconds[at : at + 8, DIM:]
        k2_scr[at : at + 8] = jnp.broadcast_to(key_two[:, None], (8, HEADS, DIM)).astype(
            jnp.bfloat16
        )
        v2_scr[at : at + 8] = jnp.broadcast_to(val_two[:, None], (8, 8, DIM))
    tile = 16
    tiles = W1 // tile
    for n, start in enumerate(starts):
        now = start // tile
        for slot in range(tiles - 1):
            source = (now + 1 + slot) % tiles
            held = cur_ref if source < now else prev_ref
            rest_scr[n, slot] = held[source * tile : (source + 1) * tile, : 2 * DIM]

    def ring_of(n, lanes, group, step):
        place = pl.multiple_of(starts[n] + group * tile, tile)
        passed = lax.broadcasted_iota(jnp.int32, (tile, DIM), 0) <= step
        own = cur_ref[pl.ds(place, tile), lanes].astype(jnp.float32)
        prev = prev_ref[pl.ds(place, tile), lanes].astype(jnp.float32)
        mixed = jnp.where(passed, own, prev).astype(jnp.bfloat16)
        whole = [rest_scr[n, slot, :, lanes] for slot in range(tiles - 1)]
        return jnp.concatenate(whole + [mixed], 0)

    def diagonal(lanes, group, step):
        zero = jnp.zeros((DIM, DIM), jnp.bfloat16)
        return jnp.concatenate(
            [
                jnp.concatenate([ring_of(0, lanes, group, step), zero], -1),
                jnp.concatenate([zero, ring_of(1, lanes, group, step)], -1),
            ],
            0,
        )

    def leave(lanes, group):
        for n, start in enumerate(starts):
            place = pl.multiple_of(start + group * tile, tile)
            rest_scr[n, group, :, lanes] = cur_ref[pl.ds(place, tile), lanes]

    def score_step(group, step, slot, first):
        local = group * tile + step
        mq = []
        for lag in range(W2):
            mq.append(
                jnp.concatenate(
                    [
                        q_scr[n * half + local] * k2_scr[n * half + local + W2 - lag]
                        for n in range(2)
                    ],
                    -1,
                )
            )
        score = lax.dot_general(
            jnp.concatenate(mq, 0), diagonal(sides[0], group, step), NT, preferred_element_type=jnp.float32
        ).reshape(W2, HEADS, 2 * DIM)
        if first:
            lag = lax.broadcasted_iota(jnp.int32, (W2, HEADS, DIM), 0)
            col = lax.broadcasted_iota(jnp.int32, (W2, HEADS, DIM), 2)
            parts = []
            for n in range(2):
                row = starts[n] + local
                seat = jnp.right_shift(col, 4)
                past = jnp.where(seat + 1 + starts[n] // tile >= tiles, 0, 1)
                past = jnp.where(seat < group, 0, past)
                past = jnp.where(seat == tiles - 1, (col & (tile - 1)) - step, past)
                allowed = (past <= 0) & (lag <= row)
                parts.append(jnp.where(allowed, score[:, :, sides[n]], NEG))
            score = jnp.concatenate(parts, -1)
        s_scr[slot] = score
        top = jnp.max(score, axis=0)
        return tuple(jnp.max(top[:, side], axis=-1, keepdims=True) for side in sides)

    def weigh_step(group, step, slot, tops):
        local = group * tile + step
        total = [None, None]
        weights = []
        for lag in range(W2):
            pair = []
            for n in range(2):
                weight = jnp.exp2((s_scr[slot, lag, :, sides[n]] - tops[n]) * EXP2_SCALE)
                total[n] = weight if lag == 0 else total[n] + weight
                pair.append(weight.astype(jnp.bfloat16))
            weights.append(jnp.concatenate(pair, -1))
        paired = jnp.dot(
            jnp.concatenate(weights, 0),
            diagonal(sides[1], group, step),
            preferred_element_type=jnp.float32,
        ).reshape(W2, 2, 8, 2 * DIM)
        for n in range(2):
            acc = None
            for lag in range(W2):
                part = paired[lag, :, :, sides[n]] * v2_scr[n * half + local + W2 - lag][None]
                acc = part if acc is None else acc + part
            result = acc.reshape(HEADS, DIM) / jnp.sum(total[n], axis=-1, keepdims=True)
            place = pl.multiple_of((n * half + local) * HEADS, HEADS)
            wide_scr[pl.ds(place, HEADS), :] = result

    def all_queries(first):
        groups = half // tile

        def one_group(group, tops):
            for step in range(tile):
                after = (group, step + 1)
                if step == tile - 1:
                    after = (jnp.minimum(group + 1, groups - 1), 0)
                    leave(sides[0], group)
                next_tops = score_step(*after, (step + 1) % 2, first)
                weigh_step(group, step, step % 2, tops)
                if step == tile - 1:
                    leave(sides[1], group)
                tops = next_tops
            return tops

        lax.fori_loop(0, groups, one_group, score_step(0, 0, 0, first))

    @pl.when(first_shard)
    def _():
        all_queries(True)

    @pl.when(jnp.logical_not(first_shard))
    def _():
        all_queries(False)

    square = jnp.zeros((rows, DIM), jnp.float32)
    for head in range(HEADS):
        result = wide_scr[pl.ds(head, rows, stride=HEADS), :].astype(jnp.bfloat16)
        out_ref[:, head * DIM : (head + 1) * DIM] = result
        wide = result.astype(jnp.float32)
        square += wide * wide
    mean = jnp.sum(square, axis=-1, keepdims=True) * (1.0 / (HEADS * DIM))
    inverse = lax.rsqrt(mean + 1e-6)
    normed = (out_ref[...].astype(jnp.float32) * inverse * gain_ref[...]).astype(jnp.bfloat16)
    kv_ref[...] = jnp.dot(
        normed, weight_ref[...], preferred_element_type=jnp.float32
    ).astype(jnp.bfloat16)


def tri_call(me, staged, tri_query, behind, tri_keys, gain, kv_weight, held, number, rows):
    token_rows, width = tri_query.shape
    whole = lambda shape: pl.BlockSpec(shape, lambda i: (0,) * len(shape))
    in_specs = [
        pl.BlockSpec(memory_space=pltpu.SMEM),
        pl.BlockSpec(memory_space=pl.ANY),
        pl.BlockSpec((rows, width), lambda i: (number, 0)),
        whole(behind.shape),
        whole(tri_keys.shape),
        whole(gain.shape),
        whole(kv_weight.shape),
    ]
    args = [me, staged, tri_query, behind, tri_keys, gain, kv_weight]
    body = functools.partial(tri_kernel, first_row=number * rows, rows=rows)
    aliases = {}
    if held is None:
        kernel = lambda *refs: body(*refs[:7], None, *refs[7:])
    else:
        kernel = body
        in_specs.append(pl.BlockSpec(memory_space=pl.ANY))
        args.append(held)
        aliases = {7: 0}
    return pl.pallas_call(
        kernel,
        grid=(1,),
        in_specs=in_specs,
        out_specs=[
            pl.BlockSpec((rows, width), lambda i: (number, 0)),
            whole((rows, 2 * DIM)),
        ],
        out_shape=[
            jax.ShapeDtypeStruct((token_rows, width), jnp.bfloat16),
            jax.ShapeDtypeStruct((rows, 2 * DIM), jnp.bfloat16),
        ],
        scratch_shapes=[
            pltpu.VMEM((rows * HEADS, DIM), jnp.float32),
            pltpu.VMEM((rows, HEADS, DIM), jnp.bfloat16),
            pltpu.VMEM((rows + W2, HEADS, DIM), jnp.bfloat16),
            pltpu.VMEM((rows + W2, 8, DIM), jnp.float32),
            pltpu.VMEM((2, W1 // 16 - 1, 16, 2 * DIM), jnp.bfloat16),
            pltpu.VMEM((2, W2, HEADS, 2 * DIM), jnp.float32),
        ],
        input_output_aliases=aliases,
        compiler_params=pltpu.CompilerParams(vmem_limit_bytes=40 * 1024 * 1024),
        cost_estimate=pl.CostEstimate(
            flops=4 * rows * HEADS * W2 * 256 * DIM, bytes_accessed=2 << 20, transcendentals=0
        ),
        name="tri_part",
    )(*args)


def stage_kernel(*refs):
    out_ref = refs[-1]
    total = jnp.zeros(out_ref.shape, jnp.float32)
    for ref in refs[:-1]:
        total += ref[0:1, 0:DIM].astype(jnp.float32)
    out_ref[...] = total


def stage_call(*arrays):
    return pl.pallas_call(
        stage_kernel,
        grid=(1,),
        in_specs=[pl.BlockSpec(a.shape, lambda i: (0, 0)) for a in arrays],
        out_specs=pl.BlockSpec((8, DIM), lambda i: (0, 0)),
        out_shape=jax.ShapeDtypeStruct((8, DIM), jnp.float32),
        compiler_params=pltpu.CompilerParams(vmem_limit_bytes=8 * 1024 * 1024),
        cost_estimate=pl.CostEstimate(flops=0, bytes_accessed=3 << 20, transcendentals=0),
        name="stage",
    )(*arrays)


SPAN = 2


def att_kernel(me_ref, q_ref, far_ref, own_ref, out_ref, s_scr, top_scr, *, rows):
    me = me_ref[0]
    shards = far_ref.shape[0] // rows + 1

    def lanes_of(head):
        return pl.ds(pl.multiple_of(head * DIM, DIM), DIM)

    def attend(before):
        tiles = before + 1
        caps = [jnp.where(tile < me, -NEG, NEG) for tile in range(before)]

        def of_tile(tile, lanes):
            if tile == before:
                return own_ref[:, lanes]
            return far_ref[tile * DIM : (tile + 1) * DIM, lanes]

        heads = max(1, min(4, shards // tiles))

        def gather_queries(item):
            return jnp.concatenate([q_ref[:, lanes_of(item * heads + h)] for h in range(heads)], 0)

        def score_step(query, slot, tile, tops):
            keys = [of_tile(tile, slice(0, DIM)), of_tile(tile + 1, slice(0, DIM))]
            both = lax.dot_general(
                query, jnp.concatenate(keys, 0), NT, preferred_element_type=jnp.float32
            )
            for h in range(heads):
                for n in range(2):
                    score = both[h * rows : (h + 1) * rows, n * DIM : (n + 1) * DIM]
                    if tile + n == before:
                        row = lax.broadcasted_iota(jnp.int32, (rows, DIM), 0)
                        col = lax.broadcasted_iota(jnp.int32, (rows, DIM), 1)
                        score = jnp.where(col <= row, score, NEG)
                    else:
                        score = jnp.minimum(score, caps[tile + n])
                    s_scr[slot, h * tiles + tile + n] = score
                    tops[h] = score if tops[h] is None else jnp.maximum(tops[h], score)

        def weigh_step(slot, tile, h, top, total, weights):
            for n in range(2):
                weight = jnp.exp2((s_scr[slot, h * tiles + tile + n] - top) * EXP2_SCALE)
                total = weight if total is None else total + weight
                weights[h].append(weight.astype(jnp.bfloat16))
            return total

        def settle(slot, tops):
            for h in range(heads):
                top = jnp.max(tops[h], axis=-1, keepdims=True)
                top_scr[slot, h] = jnp.broadcast_to(top, (rows, DIM))

        def both_steps(score_item, score_slot, weigh_item):
            query = gather_queries(score_item)
            next_tops, totals = [None] * heads, [None] * heads
            weights = [[] for _ in range(heads)]
            for tile in range(0, tiles, 2):
                score_step(query, score_slot, tile, next_tops)
                for h in range(heads):
                    top = top_scr[1 - score_slot, h]
                    totals[h] = weigh_step(1 - score_slot, tile, h, top, totals[h], weights)
            settle(score_slot, next_tops)
            values = jnp.concatenate([of_tile(t, slice(DIM, 2 * DIM)) for t in range(tiles)], 0)
            stacked = jnp.concatenate([jnp.concatenate(w, -1) for w in weights], 0)
            acc = jnp.dot(stacked, values, preferred_element_type=jnp.float32)
            for h in range(heads):
                total = jnp.sum(totals[h], axis=-1, keepdims=True)
                result = acc[h * rows : (h + 1) * rows] / total
                out_ref[:, lanes_of(weigh_item * heads + h)] = result.astype(jnp.bfloat16)

        items = HEADS // heads
        tops = [None] * heads
        query = gather_queries(0)
        for tile in range(0, tiles, 2):
            score_step(query, 0, tile, tops)
        settle(0, tops)

        def pair(k, carried):
            both_steps(2 * k + 1, 1, 2 * k)
            both_steps(jnp.minimum(2 * k + 2, items - 1), 0, 2 * k + 1)
            return carried

        lax.fori_loop(0, items // 2, pair, 0)

    lowest = 0
    for before in range(1, shards + 1, SPAN):
        chosen = (me >= lowest) & (me <= before)
        pl.when(chosen)(functools.partial(attend, before))
        lowest = before + 1


def att_call(me, att_query, far, own):
    rows, width = att_query.shape
    tokens = 16 * rows
    whole = lambda shape: pl.BlockSpec(shape, lambda i: (0,) * len(shape))
    return pl.pallas_call(
        functools.partial(att_kernel, rows=rows),
        grid=(1,),
        in_specs=[
            pl.BlockSpec(memory_space=pltpu.SMEM),
            whole(att_query.shape),
            whole(far.shape),
            whole(own.shape),
        ],
        out_specs=whole(att_query.shape),
        out_shape=jax.ShapeDtypeStruct(att_query.shape, jnp.bfloat16),
        scratch_shapes=[
            pltpu.VMEM((2, tokens // DIM, rows, DIM), jnp.float32),
            pltpu.VMEM((2, 4, rows, DIM), jnp.float32),
        ],
        compiler_params=pltpu.CompilerParams(vmem_limit_bytes=48 * 1024 * 1024),
        cost_estimate=pl.CostEstimate(
            flops=4 * rows * HEADS * tokens * DIM, bytes_accessed=3 << 20, transcendentals=0
        ),
        name="causal",
    )(me, att_query, far, own)


def passed_along(block, axis):
    count = lax.axis_size(axis)
    return lax.ppermute(block, axis, [(i, i + 1) for i in range(count - 1)])


def per_device(tri_query, tri_keys, att_query, norm_gain, kv_weight):
    rows = tri_query.shape[0]
    half = rows // 2
    shards = lax.axis_size("seq")
    me = lax.axis_index("seq")
    place = jnp.reshape(me, (1,)).astype(jnp.int32)
    gain = norm_gain.reshape(1, -1)
    behind = passed_along(tri_keys, "seq")
    staged = stage_call(tri_query, tri_keys, kv_weight)
    held, kv_late = tri_call(place, staged, tri_query, behind, tri_keys, gain, kv_weight, None, 1, half)
    before = passed_along(kv_late[half - shards :], "seq")
    tri_out, kv_early = tri_call(place, staged, tri_query, behind, tri_keys, gain, kv_weight, held, 0, half)
    own = jnp.concatenate([kv_early, kv_late], 0)
    share = lax.dynamic_slice_in_dim(jnp.concatenate([before, own], 0), shards - me, rows - 1, 0)
    far = lax.all_gather(share, "seq", axis=0, tiled=True)
    attended = att_call(place, att_query, far, own)
    return (tri_out, attended)


def solution(mesh):
    in_specs = (P(("dp", "seq"), None), P(("dp", "seq"), None), P(("dp", "seq"), None), P(), P())
    out_specs = (P(("dp", "seq"), None), P(("dp", "seq"), None))
    return jax.shard_map(
        per_device, mesh=mesh, in_specs=in_specs, out_specs=out_specs, check_vma=False
    )
```

```python
import functools

import jax
import jax.numpy as jnp
from jax import lax
from jax.experimental import pallas as pl
from jax.experimental.pallas import tpu as pltpu
from jax.sharding import PartitionSpec as P

HEADS = 16
DIM = 128
W1 = 128
W2 = 16
NEG = -1e30
SCALE = DIM**-0.5
EXP2_SCALE = SCALE * 1.4426950408889634
NT = (((1,), (1,)), ((), ()))


def tri_kernel(
    me_ref, staged_ref, q_ref, prev_ref, cur_ref, gain_ref, weight_ref, held_ref, out_ref, kv_ref,
    wide_scr, q_scr, k2_scr, v2_scr, rest_scr, s_scr, *, first_row, rows,
):
    half = rows // 2
    first_shard = me_ref[0] == 0
    starts = (first_row, first_row + half)
    sides = (slice(0, DIM), slice(DIM, 2 * DIM))

    for head in range(HEADS):
        wide_scr[pl.ds(head, rows, stride=HEADS), :] = q_ref[
            :, head * DIM : (head + 1) * DIM
        ].astype(jnp.float32)
    q_scr[...] = wide_scr[...].astype(jnp.bfloat16).reshape(rows, HEADS, DIM)
    if first_row == 0:
        seconds = [prev_ref[W1 - W2 :, 2 * DIM :], cur_ref[:rows, 2 * DIM :]]
    else:
        seconds = [cur_ref[first_row - W2 : first_row + rows, 2 * DIM :]]
    seconds = jnp.concatenate(seconds, 0).astype(jnp.float32)
    for at in range(0, rows + W2, 8):
        key_two = seconds[at : at + 8, :DIM]
        val_two = seconds[at : at + 8, DIM:]
        k2_scr[at : at + 8] = jnp.broadcast_to(key_two[:, None], (8, HEADS, DIM)).astype(
            jnp.bfloat16
        )
        v2_scr[at : at + 8] = jnp.broadcast_to(val_two[:, None], (8, 8, DIM))
    tile = 16
    tiles = W1 // tile
    for n, start in enumerate(starts):
        now = start // tile
        for slot in range(tiles - 1):
            source = (now + 1 + slot) % tiles
            held = cur_ref if source < now else prev_ref
            rest_scr[n, slot] = held[source * tile : (source + 1) * tile, : 2 * DIM]

    def ring_of(n, lanes, group, step):
        place = pl.multiple_of(starts[n] + group * tile, tile)
        passed = lax.broadcasted_iota(jnp.int32, (tile, DIM), 0) <= step
        own = cur_ref[pl.ds(place, tile), lanes].astype(jnp.float32)
        prev = prev_ref[pl.ds(place, tile), lanes].astype(jnp.float32)
        mixed = jnp.where(passed, own, prev).astype(jnp.bfloat16)
        whole = [rest_scr[n, slot, :, lanes] for slot in range(tiles - 1)]
        return jnp.concatenate(whole + [mixed], 0)

    def diagonal(lanes, group, step):
        zero = jnp.zeros((DIM, DIM), jnp.bfloat16)
        return jnp.concatenate(
            [
                jnp.concatenate([ring_of(0, lanes, group, step), zero], -1),
                jnp.concatenate([zero, ring_of(1, lanes, group, step)], -1),
            ],
            0,
        )

    def leave(lanes, group):
        for n, start in enumerate(starts):
            place = pl.multiple_of(start + group * tile, tile)
            rest_scr[n, group, :, lanes] = cur_ref[pl.ds(place, tile), lanes]

    def score_step(group, step, slot, first):
        local = group * tile + step
        mq = []
        for lag in range(W2):
            mq.append(
                jnp.concatenate(
                    [
                        q_scr[n * half + local] * k2_scr[n * half + local + W2 - lag]
                        for n in range(2)
                    ],
                    -1,
                )
            )
        score = lax.dot_general(
            jnp.concatenate(mq, 0), diagonal(sides[0], group, step), NT, preferred_element_type=jnp.float32
        ).reshape(W2, HEADS, 2 * DIM)
        if first:
            lag = lax.broadcasted_iota(jnp.int32, (W2, HEADS, DIM), 0)
            col = lax.broadcasted_iota(jnp.int32, (W2, HEADS, DIM), 2)
            parts = []
            for n in range(2):
                row = starts[n] + local
                seat = jnp.right_shift(col, 4)
                past = jnp.where(seat + 1 + starts[n] // tile >= tiles, 0, 1)
                past = jnp.where(seat < group, 0, past)
                past = jnp.where(seat == tiles - 1, (col & (tile - 1)) - step, past)
                allowed = (past <= 0) & (lag <= row)
                parts.append(jnp.where(allowed, score[:, :, sides[n]], NEG))
            score = jnp.concatenate(parts, -1)
        s_scr[slot] = score
        top = jnp.max(score, axis=0)
        return tuple(jnp.max(top[:, side], axis=-1, keepdims=True) for side in sides)

    def weigh_step(group, step, slot, tops):
        local = group * tile + step
        total = [None, None]
        weights = []
        for lag in range(W2):
            pair = []
            for n in range(2):
                weight = jnp.exp2((s_scr[slot, lag, :, sides[n]] - tops[n]) * EXP2_SCALE)
                total[n] = weight if lag == 0 else total[n] + weight
                pair.append(weight.astype(jnp.bfloat16))
            weights.append(jnp.concatenate(pair, -1))
        paired = jnp.dot(
            jnp.concatenate(weights, 0),
            diagonal(sides[1], group, step),
            preferred_element_type=jnp.float32,
        ).reshape(W2, 2, 8, 2 * DIM)
        for n in range(2):
            acc = None
            for lag in range(W2):
                part = paired[lag, :, :, sides[n]] * v2_scr[n * half + local + W2 - lag][None]
                acc = part if acc is None else acc + part
            result = acc.reshape(HEADS, DIM) / jnp.sum(total[n], axis=-1, keepdims=True)
            place = pl.multiple_of((n * half + local) * HEADS, HEADS)
            wide_scr[pl.ds(place, HEADS), :] = result

    def all_queries(first):
        groups = half // tile

        def one_group(group, tops):
            for step in range(tile):
                after = (group, step + 1)
                if step == tile - 1:
                    after = (jnp.minimum(group + 1, groups - 1), 0)
                    leave(sides[0], group)
                next_tops = score_step(*after, (step + 1) % 2, first)
                weigh_step(group, step, step % 2, tops)
                if step == tile - 1:
                    leave(sides[1], group)
                tops = next_tops
            return tops

        lax.fori_loop(0, groups, one_group, score_step(0, 0, 0, first))

    @pl.when(first_shard)
    def _():
        all_queries(True)

    @pl.when(jnp.logical_not(first_shard))
    def _():
        all_queries(False)

    square = jnp.zeros((rows, DIM), jnp.float32)
    for head in range(HEADS):
        result = wide_scr[pl.ds(head, rows, stride=HEADS), :].astype(jnp.bfloat16)
        out_ref[:, head * DIM : (head + 1) * DIM] = result
        wide = result.astype(jnp.float32)
        square += wide * wide
    mean = jnp.sum(square, axis=-1, keepdims=True) * (1.0 / (HEADS * DIM))
    inverse = lax.rsqrt(mean + 1e-6)
    normed = (out_ref[...].astype(jnp.float32) * inverse * gain_ref[...]).astype(jnp.bfloat16)
    kv_ref[...] = jnp.dot(
        normed, weight_ref[...], preferred_element_type=jnp.float32
    ).astype(jnp.bfloat16)


def tri_call(me, staged, tri_query, behind, tri_keys, gain, kv_weight, held, number, rows, relayed=None):
    token_rows, width = tri_query.shape
    whole = lambda shape: pl.BlockSpec(shape, lambda i: (0,) * len(shape))
    in_specs = [
        pl.BlockSpec(memory_space=pltpu.SMEM),
        pl.BlockSpec(memory_space=pl.ANY),
        pl.BlockSpec((rows, width), lambda i: (number, 0)),
        whole(behind.shape),
        whole(tri_keys.shape),
        whole(gain.shape),
        whole(kv_weight.shape),
    ]
    args = [me, staged, tri_query, behind, tri_keys, gain, kv_weight]
    body = functools.partial(tri_kernel, first_row=number * rows, rows=rows)
    aliases = {}
    more_specs, more_shapes, more_scratch = [], [], []
    if held is None:
        kernel = lambda *refs: body(*refs[:7], None, *refs[7:])
    else:

        def kernel(*refs):
            copy = pltpu.make_async_copy(refs[8], refs[11], refs[-1])
            copy.start()
            body(*refs[:8], *refs[9:11], *refs[12:-1])
            copy.wait()

        in_specs.append(pl.BlockSpec(memory_space=pl.ANY))
        in_specs.append(pl.BlockSpec(memory_space=pltpu.HBM))
        args += [held, relayed]
        aliases = {7: 0}
        more_specs = [pl.BlockSpec(memory_space=pl.ANY)]
        more_shapes = [jax.ShapeDtypeStruct(relayed.shape, relayed.dtype)]
        more_scratch = [pltpu.SemaphoreType.DMA]
    return pl.pallas_call(
        kernel,
        grid=(1,),
        in_specs=in_specs,
        out_specs=[
            pl.BlockSpec((rows, width), lambda i: (number, 0)),
            whole((rows, 2 * DIM)),
            *more_specs,
        ],
        out_shape=[
            jax.ShapeDtypeStruct((token_rows, width), jnp.bfloat16),
            jax.ShapeDtypeStruct((rows, 2 * DIM), jnp.bfloat16),
            *more_shapes,
        ],
        scratch_shapes=[
            pltpu.VMEM((rows * HEADS, DIM), jnp.float32),
            pltpu.VMEM((rows, HEADS, DIM), jnp.bfloat16),
            pltpu.VMEM((rows + W2, HEADS, DIM), jnp.bfloat16),
            pltpu.VMEM((rows + W2, 8, DIM), jnp.float32),
            pltpu.VMEM((2, W1 // 16 - 1, 16, 2 * DIM), jnp.bfloat16),
            pltpu.VMEM((2, W2, HEADS, 2 * DIM), jnp.float32),
            *more_scratch,
        ],
        input_output_aliases=aliases,
        compiler_params=pltpu.CompilerParams(vmem_limit_bytes=40 * 1024 * 1024),
        cost_estimate=pl.CostEstimate(
            flops=4 * rows * HEADS * W2 * 256 * DIM, bytes_accessed=2 << 20, transcendentals=0
        ),
        name="tri_part",
    )(*args)


def stage_kernel(*refs):
    out_ref = refs[-1]
    total = jnp.zeros(out_ref.shape, jnp.float32)
    for ref in refs[:-1]:
        total += ref[0:1, 0:DIM].astype(jnp.float32)
    out_ref[...] = total


def stage_call(*arrays):
    return pl.pallas_call(
        stage_kernel,
        grid=(1,),
        in_specs=[pl.BlockSpec(a.shape, lambda i: (0, 0)) for a in arrays],
        out_specs=pl.BlockSpec((8, DIM), lambda i: (0, 0)),
        out_shape=jax.ShapeDtypeStruct((8, DIM), jnp.float32),
        compiler_params=pltpu.CompilerParams(vmem_limit_bytes=8 * 1024 * 1024),
        cost_estimate=pl.CostEstimate(flops=0, bytes_accessed=3 << 20, transcendentals=0),
        name="stage",
    )(*arrays)


SPAN = 2


def att_kernel(me_ref, q_ref, far_ref, own_ref, out_ref, s_scr, top_scr, *, rows):
    me = me_ref[0]
    shards = far_ref.shape[0] // rows + 1

    def lanes_of(head):
        return pl.ds(pl.multiple_of(head * DIM, DIM), DIM)

    def attend(before):
        tiles = before + 1
        caps = [jnp.where(tile < me, -NEG, NEG) for tile in range(before)]

        def of_tile(tile, lanes):
            if tile == before:
                return own_ref[:, lanes]
            return far_ref[tile * DIM : (tile + 1) * DIM, lanes]

        heads = max(1, min(4, shards // tiles))

        def gather_queries(item):
            return jnp.concatenate([q_ref[:, lanes_of(item * heads + h)] for h in range(heads)], 0)

        def score_step(query, slot, tile, tops):
            keys = [of_tile(tile, slice(0, DIM)), of_tile(tile + 1, slice(0, DIM))]
            both = lax.dot_general(
                query, jnp.concatenate(keys, 0), NT, preferred_element_type=jnp.float32
            )
            for h in range(heads):
                for n in range(2):
                    score = both[h * rows : (h + 1) * rows, n * DIM : (n + 1) * DIM]
                    if tile + n == before:
                        row = lax.broadcasted_iota(jnp.int32, (rows, DIM), 0)
                        col = lax.broadcasted_iota(jnp.int32, (rows, DIM), 1)
                        score = jnp.where(col <= row, score, NEG)
                    else:
                        score = jnp.minimum(score, caps[tile + n])
                    s_scr[slot, h * tiles + tile + n] = score
                    tops[h] = score if tops[h] is None else jnp.maximum(tops[h], score)

        def weigh_step(slot, tile, h, top, total, weights):
            for n in range(2):
                weight = jnp.exp2((s_scr[slot, h * tiles + tile + n] - top) * EXP2_SCALE)
                total = weight if total is None else total + weight
                weights[h].append(weight.astype(jnp.bfloat16))
            return total

        def settle(slot, tops):
            for h in range(heads):
                top = jnp.max(tops[h], axis=-1, keepdims=True)
                top_scr[slot, h] = jnp.broadcast_to(top, (rows, DIM))

        def both_steps(score_item, score_slot, weigh_item):
            query = gather_queries(score_item)
            next_tops, totals = [None] * heads, [None] * heads
            weights = [[] for _ in range(heads)]
            for tile in range(0, tiles, 2):
                score_step(query, score_slot, tile, next_tops)
                for h in range(heads):
                    top = top_scr[1 - score_slot, h]
                    totals[h] = weigh_step(1 - score_slot, tile, h, top, totals[h], weights)
            settle(score_slot, next_tops)
            values = jnp.concatenate([of_tile(t, slice(DIM, 2 * DIM)) for t in range(tiles)], 0)
            stacked = jnp.concatenate([jnp.concatenate(w, -1) for w in weights], 0)
            acc = jnp.dot(stacked, values, preferred_element_type=jnp.float32)
            for h in range(heads):
                total = jnp.sum(totals[h], axis=-1, keepdims=True)
                result = acc[h * rows : (h + 1) * rows] / total
                out_ref[:, lanes_of(weigh_item * heads + h)] = result.astype(jnp.bfloat16)

        items = HEADS // heads
        tops = [None] * heads
        query = gather_queries(0)
        for tile in range(0, tiles, 2):
            score_step(query, 0, tile, tops)
        settle(0, tops)

        def pair(k, carried):
            both_steps(2 * k + 1, 1, 2 * k)
            both_steps(jnp.minimum(2 * k + 2, items - 1), 0, 2 * k + 1)
            return carried

        lax.fori_loop(0, items // 2, pair, 0)

    lowest = 0
    for before in range(1, shards + 1, SPAN):
        chosen = (me >= lowest) & (me <= before)
        pl.when(chosen)(functools.partial(attend, before))
        lowest = before + 1


def att_call(me, att_query, far, own):
    rows, width = att_query.shape
    tokens = 16 * rows
    whole = lambda shape: pl.BlockSpec(shape, lambda i: (0,) * len(shape))
    return pl.pallas_call(
        functools.partial(att_kernel, rows=rows),
        grid=(1,),
        in_specs=[
            pl.BlockSpec(memory_space=pltpu.SMEM),
            whole(att_query.shape),
            whole(far.shape),
            whole(own.shape),
        ],
        out_specs=whole(att_query.shape),
        out_shape=jax.ShapeDtypeStruct(att_query.shape, jnp.bfloat16),
        scratch_shapes=[
            pltpu.VMEM((2, tokens // DIM, rows, DIM), jnp.float32),
            pltpu.VMEM((2, 4, rows, DIM), jnp.float32),
        ],
        compiler_params=pltpu.CompilerParams(vmem_limit_bytes=48 * 1024 * 1024),
        cost_estimate=pl.CostEstimate(
            flops=4 * rows * HEADS * tokens * DIM, bytes_accessed=3 << 20, transcendentals=0
        ),
        name="causal",
    )(me, att_query, far, own)


def passed_along(block, axis):
    count = lax.axis_size(axis)
    return lax.ppermute(block, axis, [(i, i + 1) for i in range(count - 1)])


def per_device(tri_query, tri_keys, att_query, norm_gain, kv_weight):
    rows = tri_query.shape[0]
    half = rows // 2
    shards = lax.axis_size("seq")
    me = lax.axis_index("seq")
    place = jnp.reshape(me, (1,)).astype(jnp.int32)
    gain = norm_gain.reshape(1, -1)
    behind = passed_along(tri_keys, "seq")
    staged = stage_call(tri_query, tri_keys, gain, kv_weight)
    held, kv_late = tri_call(place, staged, tri_query, behind, tri_keys, gain, kv_weight, None, 1, half)
    before = passed_along(kv_late[half - shards :], "seq")
    tri_out, kv_early, near_query = tri_call(
        place, staged, tri_query, behind, tri_keys, gain, kv_weight, held, 0, half, att_query
    )
    own = jnp.concatenate([kv_early, kv_late], 0)
    share = lax.dynamic_slice_in_dim(jnp.concatenate([before, own], 0), shards - me, rows - 1, 0)
    far = lax.all_gather(share, "seq", axis=0, tiled=True)
    attended = att_call(place, near_query, far, own)
    return (tri_out, attended)


def solution(mesh):
    in_specs = (P(("dp", "seq"), None), P(("dp", "seq"), None), P(("dp", "seq"), None), P(), P())
    out_specs = (P(("dp", "seq"), None), P(("dp", "seq"), None))
    return jax.shard_map(
        per_device, mesh=mesh, in_specs=in_specs, out_specs=out_specs, check_vma=False
    )
```

```python
import functools

import jax
import jax.numpy as jnp
from jax import lax
from jax.experimental import pallas as pl
from jax.experimental.pallas import tpu as pltpu
from jax.sharding import PartitionSpec as P

HEADS = 16
DIM = 128
W1 = 128
W2 = 16
NEG = -1e30
SCALE = DIM**-0.5
EXP2_SCALE = SCALE * 1.4426950408889634
NT = (((1,), (1,)), ((), ()))


def tri_kernel(
    me_ref, staged_ref, q_ref, prev_ref, cur_ref, gain_ref, weight_ref, held_ref, out_ref, kv_ref,
    wide_scr, q_scr, k2_scr, v2_scr, rest_scr, s_scr, *, first_row, rows,
):
    half = rows // 2
    first_shard = me_ref[0] == 0
    starts = (first_row, first_row + half)
    sides = (slice(0, DIM), slice(DIM, 2 * DIM))

    for head in range(HEADS):
        wide_scr[pl.ds(head, rows, stride=HEADS), :] = q_ref[
            :, head * DIM : (head + 1) * DIM
        ].astype(jnp.float32)
    q_scr[...] = wide_scr[...].astype(jnp.bfloat16).reshape(rows, HEADS, DIM)
    if first_row == 0:
        seconds = [prev_ref[W1 - W2 :, 2 * DIM :], cur_ref[:rows, 2 * DIM :]]
    else:
        seconds = [cur_ref[first_row - W2 : first_row + rows, 2 * DIM :]]
    seconds = jnp.concatenate(seconds, 0).astype(jnp.float32)
    for at in range(0, rows + W2, 8):
        key_two = seconds[at : at + 8, :DIM]
        val_two = seconds[at : at + 8, DIM:]
        k2_scr[at : at + 8] = jnp.broadcast_to(key_two[:, None], (8, HEADS, DIM)).astype(
            jnp.bfloat16
        )
        v2_scr[at : at + 8] = jnp.broadcast_to(val_two[:, None], (8, 8, DIM))
    tile = 16
    tiles = W1 // tile
    for n, start in enumerate(starts):
        now = start // tile
        for slot in range(tiles - 1):
            source = (now + 1 + slot) % tiles
            held = cur_ref if source < now else prev_ref
            rest_scr[n, slot] = held[source * tile : (source + 1) * tile, : 2 * DIM]

    def ring_of(n, lanes, group, step):
        place = pl.multiple_of(starts[n] + group * tile, tile)
        passed = lax.broadcasted_iota(jnp.int32, (tile, DIM), 0) <= step
        own = cur_ref[pl.ds(place, tile), lanes].astype(jnp.float32)
        prev = prev_ref[pl.ds(place, tile), lanes].astype(jnp.float32)
        mixed = jnp.where(passed, own, prev).astype(jnp.bfloat16)
        whole = [rest_scr[n, slot, :, lanes] for slot in range(tiles - 1)]
        return jnp.concatenate(whole + [mixed], 0)

    def diagonal(lanes, group, step):
        zero = jnp.zeros((DIM, DIM), jnp.bfloat16)
        return jnp.concatenate(
            [
                jnp.concatenate([ring_of(0, lanes, group, step), zero], -1),
                jnp.concatenate([zero, ring_of(1, lanes, group, step)], -1),
            ],
            0,
        )

    def leave(lanes, group):
        for n, start in enumerate(starts):
            place = pl.multiple_of(start + group * tile, tile)
            rest_scr[n, group, :, lanes] = cur_ref[pl.ds(place, tile), lanes]

    def score_step(group, step, slot, first):
        local = group * tile + step
        mq = []
        for lag in range(W2):
            mq.append(
                jnp.concatenate(
                    [
                        q_scr[n * half + local] * k2_scr[n * half + local + W2 - lag]
                        for n in range(2)
                    ],
                    -1,
                )
            )
        score = lax.dot_general(
            jnp.concatenate(mq, 0), diagonal(sides[0], group, step), NT, preferred_element_type=jnp.float32
        ).reshape(W2, HEADS, 2 * DIM)
        if first:
            lag = lax.broadcasted_iota(jnp.int32, (W2, HEADS, DIM), 0)
            col = lax.broadcasted_iota(jnp.int32, (W2, HEADS, DIM), 2)
            parts = []
            for n in range(2):
                row = starts[n] + local
                seat = jnp.right_shift(col, 4)
                past = jnp.where(seat + 1 + starts[n] // tile >= tiles, 0, 1)
                past = jnp.where(seat < group, 0, past)
                past = jnp.where(seat == tiles - 1, (col & (tile - 1)) - step, past)
                allowed = (past <= 0) & (lag <= row)
                parts.append(jnp.where(allowed, score[:, :, sides[n]], NEG))
            score = jnp.concatenate(parts, -1)
        s_scr[slot] = score
        top = jnp.max(score, axis=0)
        return tuple(jnp.max(top[:, side], axis=-1, keepdims=True) for side in sides)

    def weigh_step(group, step, slot, tops):
        local = group * tile + step
        total = [None, None]
        weights = []
        for lag in range(W2):
            pair = []
            for n in range(2):
                weight = jnp.exp2((s_scr[slot, lag, :, sides[n]] - tops[n]) * EXP2_SCALE)
                total[n] = weight if lag == 0 else total[n] + weight
                pair.append(weight.astype(jnp.bfloat16))
            weights.append(jnp.concatenate(pair, -1))
        paired = jnp.dot(
            jnp.concatenate(weights, 0),
            diagonal(sides[1], group, step),
            preferred_element_type=jnp.float32,
        ).reshape(W2, 2, 8, 2 * DIM)
        for n in range(2):
            acc = None
            for lag in range(W2):
                part = paired[lag, :, :, sides[n]] * v2_scr[n * half + local + W2 - lag][None]
                acc = part if acc is None else acc + part
            result = acc.reshape(HEADS, DIM) / jnp.sum(total[n], axis=-1, keepdims=True)
            place = pl.multiple_of((n * half + local) * HEADS, HEADS)
            wide_scr[pl.ds(place, HEADS), :] = result

    def all_queries(first):
        groups = half // tile

        def one_group(group, tops):
            for step in range(tile):
                after = (group, step + 1)
                if step == tile - 1:
                    after = (jnp.minimum(group + 1, groups - 1), 0)
                    leave(sides[0], group)
                next_tops = score_step(*after, (step + 1) % 2, first)
                weigh_step(group, step, step % 2, tops)
                if step == tile - 1:
                    leave(sides[1], group)
                tops = next_tops
            return tops

        lax.fori_loop(0, groups, one_group, score_step(0, 0, 0, first))

    @pl.when(first_shard)
    def _():
        all_queries(True)

    @pl.when(jnp.logical_not(first_shard))
    def _():
        all_queries(False)

    square = jnp.zeros((rows, DIM), jnp.float32)
    for head in range(HEADS):
        result = wide_scr[pl.ds(head, rows, stride=HEADS), :].astype(jnp.bfloat16)
        out_ref[:, head * DIM : (head + 1) * DIM] = result
        wide = result.astype(jnp.float32)
        square += wide * wide
    mean = jnp.sum(square, axis=-1, keepdims=True) * (1.0 / (HEADS * DIM))
    inverse = lax.rsqrt(mean + 1e-6)
    normed = (out_ref[...].astype(jnp.float32) * inverse * gain_ref[...]).astype(jnp.bfloat16)
    kv_ref[...] = jnp.dot(
        normed, weight_ref[...], preferred_element_type=jnp.float32
    ).astype(jnp.bfloat16)


def tri_call(me, staged, tri_query, behind, tri_keys, gain, kv_weight, held, number, rows, relayed=None):
    token_rows, width = tri_query.shape
    whole = lambda shape: pl.BlockSpec(shape, lambda i: (0,) * len(shape))
    in_specs = [
        pl.BlockSpec(memory_space=pltpu.SMEM),
        pl.BlockSpec(memory_space=pl.ANY),
        pl.BlockSpec((rows, width), lambda i: (number, 0)),
        whole(behind.shape),
        whole(tri_keys.shape),
        whole(gain.shape),
        whole(kv_weight.shape),
    ]
    args = [me, staged, tri_query, behind, tri_keys, gain, kv_weight]
    body = functools.partial(tri_kernel, first_row=number * rows, rows=rows)
    aliases = {}
    more_specs, more_shapes, more_scratch = [], [], []
    if held is None:
        kernel = lambda *refs: body(*refs[:7], None, *refs[7:])
    else:

        def kernel(*refs):
            copy = pltpu.make_async_copy(refs[8], refs[11], refs[-1])
            copy.start()
            body(*refs[:8], *refs[9:11], *refs[12:-1])
            copy.wait()

        in_specs.append(pl.BlockSpec(memory_space=pl.ANY))
        in_specs.append(pl.BlockSpec(memory_space=pltpu.HBM))
        args += [held, relayed]
        aliases = {7: 0}
        more_specs = [pl.BlockSpec(memory_space=pl.ANY)]
        more_shapes = [jax.ShapeDtypeStruct(relayed.shape, relayed.dtype)]
        more_scratch = [pltpu.SemaphoreType.DMA]
    return pl.pallas_call(
        kernel,
        grid=(1,),
        in_specs=in_specs,
        out_specs=[
            pl.BlockSpec((rows, width), lambda i: (number, 0)),
            whole((rows, 2 * DIM)),
            *more_specs,
        ],
        out_shape=[
            jax.ShapeDtypeStruct((token_rows, width), jnp.bfloat16),
            jax.ShapeDtypeStruct((rows, 2 * DIM), jnp.bfloat16),
            *more_shapes,
        ],
        scratch_shapes=[
            pltpu.VMEM((rows * HEADS, DIM), jnp.float32),
            pltpu.VMEM((rows, HEADS, DIM), jnp.bfloat16),
            pltpu.VMEM((rows + W2, HEADS, DIM), jnp.bfloat16),
            pltpu.VMEM((rows + W2, 8, DIM), jnp.float32),
            pltpu.VMEM((2, W1 // 16 - 1, 16, 2 * DIM), jnp.bfloat16),
            pltpu.VMEM((2, W2, HEADS, 2 * DIM), jnp.float32),
            *more_scratch,
        ],
        input_output_aliases=aliases,
        compiler_params=pltpu.CompilerParams(vmem_limit_bytes=40 * 1024 * 1024),
        cost_estimate=pl.CostEstimate(
            flops=4 * rows * HEADS * W2 * 256 * DIM, bytes_accessed=2 << 20, transcendentals=0
        ),
        name="tri_part",
    )(*args)


def stage_kernel(*refs):
    out_ref = refs[-1]
    total = jnp.zeros(out_ref.shape, jnp.float32)
    for ref in refs[:-1]:
        total += ref[0:1, 0:DIM].astype(jnp.float32)
    out_ref[...] = total


def stage_call(*arrays):
    return pl.pallas_call(
        stage_kernel,
        grid=(1,),
        in_specs=[pl.BlockSpec(a.shape, lambda i: (0, 0)) for a in arrays],
        out_specs=pl.BlockSpec((8, DIM), lambda i: (0, 0)),
        out_shape=jax.ShapeDtypeStruct((8, DIM), jnp.float32),
        compiler_params=pltpu.CompilerParams(vmem_limit_bytes=8 * 1024 * 1024),
        cost_estimate=pl.CostEstimate(flops=0, bytes_accessed=3 << 20, transcendentals=0),
        name="stage",
    )(*arrays)


SPAN = 2


def att_kernel(me_ref, q_ref, far_ref, own_ref, out_ref, s_scr, top_scr, *, rows):
    me = me_ref[0]
    shards = far_ref.shape[0] // rows + 1

    def lanes_of(head):
        return pl.ds(pl.multiple_of(head * DIM, DIM), DIM)

    def attend(before):
        tiles = before + 1
        caps = [jnp.where(tile < me, -NEG, NEG) for tile in range(before)]

        def of_tile(tile, lanes):
            if tile == before:
                return own_ref[:, lanes]
            return far_ref[tile * DIM : (tile + 1) * DIM, lanes]

        heads = max(1, min(8, shards // tiles))

        def gather_queries(item):
            return jnp.concatenate([q_ref[:, lanes_of(item * heads + h)] for h in range(heads)], 0)

        def score_step(query, slot, tile, tops):
            keys = [of_tile(tile, slice(0, DIM)), of_tile(tile + 1, slice(0, DIM))]
            both = lax.dot_general(
                query, jnp.concatenate(keys, 0), NT, preferred_element_type=jnp.float32
            )
            for h in range(heads):
                for n in range(2):
                    score = both[h * rows : (h + 1) * rows, n * DIM : (n + 1) * DIM]
                    if tile + n == before:
                        row = lax.broadcasted_iota(jnp.int32, (rows, DIM), 0)
                        col = lax.broadcasted_iota(jnp.int32, (rows, DIM), 1)
                        score = jnp.where(col <= row, score, NEG)
                    else:
                        score = jnp.minimum(score, caps[tile + n])
                    s_scr[slot, h * tiles + tile + n] = score
                    tops[h] = score if tops[h] is None else jnp.maximum(tops[h], score)

        def weigh_step(slot, tile, h, top, total, weights):
            for n in range(2):
                weight = jnp.exp2((s_scr[slot, h * tiles + tile + n] - top) * EXP2_SCALE)
                total = weight if total is None else total + weight
                weights[h].append(weight.astype(jnp.bfloat16))
            return total

        def settle(slot, tops):
            for h in range(heads):
                top = jnp.max(tops[h], axis=-1, keepdims=True)
                top_scr[slot, h] = jnp.broadcast_to(top, (rows, DIM))

        def both_steps(score_item, score_slot, weigh_item):
            query = gather_queries(score_item)
            next_tops, totals = [None] * heads, [None] * heads
            weights = [[] for _ in range(heads)]
            for tile in range(0, tiles, 2):
                score_step(query, score_slot, tile, next_tops)
                for h in range(heads):
                    top = top_scr[1 - score_slot, h]
                    totals[h] = weigh_step(1 - score_slot, tile, h, top, totals[h], weights)
            settle(score_slot, next_tops)
            values = jnp.concatenate([of_tile(t, slice(DIM, 2 * DIM)) for t in range(tiles)], 0)
            stacked = jnp.concatenate([jnp.concatenate(w, -1) for w in weights], 0)
            acc = jnp.dot(stacked, values, preferred_element_type=jnp.float32)
            for h in range(heads):
                total = jnp.sum(totals[h], axis=-1, keepdims=True)
                result = acc[h * rows : (h + 1) * rows] / total
                out_ref[:, lanes_of(weigh_item * heads + h)] = result.astype(jnp.bfloat16)

        items = HEADS // heads
        tops = [None] * heads
        query = gather_queries(0)
        for tile in range(0, tiles, 2):
            score_step(query, 0, tile, tops)
        settle(0, tops)

        def pair(k, carried):
            both_steps(2 * k + 1, 1, 2 * k)
            both_steps(jnp.minimum(2 * k + 2, items - 1), 0, 2 * k + 1)
            return carried

        lax.fori_loop(0, items // 2, pair, 0)

    lowest = 0
    for before in range(1, shards + 1, SPAN):
        chosen = (me >= lowest) & (me <= before)
        pl.when(chosen)(functools.partial(attend, before))
        lowest = before + 1


def att_call(me, att_query, far, own):
    rows, width = att_query.shape
    tokens = 16 * rows
    whole = lambda shape: pl.BlockSpec(shape, lambda i: (0,) * len(shape))
    return pl.pallas_call(
        functools.partial(att_kernel, rows=rows),
        grid=(1,),
        in_specs=[
            pl.BlockSpec(memory_space=pltpu.SMEM),
            whole(att_query.shape),
            whole(far.shape),
            whole(own.shape),
        ],
        out_specs=whole(att_query.shape),
        out_shape=jax.ShapeDtypeStruct(att_query.shape, jnp.bfloat16),
        scratch_shapes=[
            pltpu.VMEM((2, tokens // DIM, rows, DIM), jnp.float32),
            pltpu.VMEM((2, 8, rows, DIM), jnp.float32),
        ],
        compiler_params=pltpu.CompilerParams(vmem_limit_bytes=48 * 1024 * 1024),
        cost_estimate=pl.CostEstimate(
            flops=4 * rows * HEADS * tokens * DIM, bytes_accessed=3 << 20, transcendentals=0
        ),
        name="causal",
    )(me, att_query, far, own)


def passed_along(block, axis):
    count = lax.axis_size(axis)
    return lax.ppermute(block, axis, [(i, i + 1) for i in range(count - 1)])


def per_device(tri_query, tri_keys, att_query, norm_gain, kv_weight):
    rows = tri_query.shape[0]
    half = rows // 2
    shards = lax.axis_size("seq")
    me = lax.axis_index("seq")
    place = jnp.reshape(me, (1,)).astype(jnp.int32)
    gain = norm_gain.reshape(1, -1)
    behind = passed_along(tri_keys, "seq")
    staged = stage_call(tri_query, tri_keys, gain, kv_weight)
    held, kv_late = tri_call(place, staged, tri_query, behind, tri_keys, gain, kv_weight, None, 1, half)
    before = passed_along(kv_late[half - shards :], "seq")
    tri_out, kv_early, near_query = tri_call(
        place, staged, tri_query, behind, tri_keys, gain, kv_weight, held, 0, half, att_query
    )
    own = jnp.concatenate([kv_early, kv_late], 0)
    share = lax.dynamic_slice_in_dim(jnp.concatenate([before, own], 0), shards - me, rows - 1, 0)
    far = lax.all_gather(share, "seq", axis=0, tiled=True)
    attended = att_call(place, near_query, far, own)
    return (tri_out, attended)


def solution(mesh):
    in_specs = (P(("dp", "seq"), None), P(("dp", "seq"), None), P(("dp", "seq"), None), P(), P())
    out_specs = (P(("dp", "seq"), None), P(("dp", "seq"), None))
    return jax.shard_map(
        per_device, mesh=mesh, in_specs=in_specs, out_specs=out_specs, check_vma=False
    )
```
